256 devices in a mesh: paper: 32 (over x_lo, z, core), type: 8 (over y, x_hi).
Axes of the slice: x: 4 (x_hi: 2, x_lo: 2; x = x_hi * 2 + x_lo), y: 4, z: 8, core: 2. Of those that a mesh axis runs over, the one named last changes fastest.
Arguments:
- papers: bfloat16 [131072, 512], P(('paper', 'type')), may hold values from -6 to 6
- cited_rows: bfloat16 [4096, 512], P('paper'), may hold values from -6 to 6
- entities: bfloat16 [1024, 512], P('type'), may hold values from -6 to 6
- entity_kinds: int32 [1024], P('type'), may hold values from 0 to 1
- query_weight: bfloat16 [512, 512], replicated, may hold values from -0.25 to 0.25
- key_weight: bfloat16 [3, 512, 512], replicated, may hold values from -0.25 to 0.25
- value_weight: bfloat16 [3, 512, 512], replicated, may hold values from -0.25 to 0.25
- attention_rel: bfloat16 [4, 8, 64, 64], replicated, may hold values from -0.75 to 0.75
- message_rel: bfloat16 [4, 8, 64, 64], replicated, may hold values from -0.75 to 0.75
- relation_prior: float32 [4, 8], replicated, may hold values from 0.5 to 2.5
- output_weight: bfloat16 [512, 512], replicated, may hold values from -0.25 to 0.25
- skip_gate: float32 [1], replicated, may hold values from -1 to 1
- norm_gain: float32 [512], replicated, may hold values from 0.5 to 1.5
- cite_pattern: int32 [1024, 8, 128, 128], P(('paper', 'type')), may hold values from 0 to 1, as said below
- cite_tiles: int32 [1024, 8], P(('paper', 'type')), may hold values from 0 to 31, as said below
- cite_counts: int32 [1024, 8], P(('paper', 'type')), may hold values from 0 to 16384, as said below
- entity_pattern: int32 [1024, 2, 128, 128], P(('paper', 'type')), may hold values from 0 to 1, as said below
- entity_tiles: int32 [1024, 2], P(('paper', 'type')), may hold values from 0 to 7, as said below
- entity_counts: int32 [1024, 2], P(('paper', 'type')), may hold values from 0 to 16384, as said below
Outputs:
- updated: bfloat16 [131072, 512], P(('paper', 'type'))
The draws below stay inside these ranges and needn't reach their ends.
Inputs may be any that keep to these rules, and one draw needn't show every extreme that they name: `cite_pattern`: entry [a, k, p, c] is 1 where paper 128 * a + p has an edge from source 128 * cite_tiles[a, k] + c, else 0. A tile of papers uses its first 8, 4, 2 or 1 slots (at least one), the same number for all tiles of one device's papers; later slots are all zero. `cite_tiles`: the slots of one tile name distinct tiles. `cite_counts`: the number of ones in the slot's block. `entity_pattern`: as cite_pattern, with sources 128 * entity_tiles[a, k] + c; a tile uses its first 1 to 2 slots, later slots are all zero. `entity_tiles`: the slots of one tile name distinct tiles. `entity_counts`: the number of ones in the slot's block.
All inputs are finite; a program needn't handle non-finite values.
Results may differ from the reference program's by a relative error of at most 0.0087.
Values may be sent and summed in bfloat16 or wider, within the bound.
No kernel may reach another device: no remote copies, remote signals or barrier semaphores. Data moves between devices by JAX's collectives and lax.ppermute only.
A program may use at most 128 MiB of HBM per device.

```python
import math
import jax
import jax.numpy as jnp
from jax import lax

D = 512
HEADS = 8
HEAD_DIM = 64
TILE = 128
K_CITE = 8
K_ENT = 2
T_DEV = 512
TARGETS = 131072
CITED = 4096
ENTITIES = 1024
TILES = 1024


def block_draw(key, salt, tile_count, slot_count, source_count, tile_size, group_size, halving):
    key = jax.random.fold_in(key, salt)
    key_order, key_level, key_bits = jax.random.split(key, 3)
    ranking = jax.random.randint(key_order, (tile_count, source_count), 0, 1 << 20, dtype=jnp.int32) * source_count
    ranking = ranking + jnp.arange(source_count, dtype=jnp.int32)[None, :]
    columns = jnp.argsort(ranking, axis=1)[:, :slot_count].astype(jnp.int32)
    if halving:
        levels = jax.random.randint(key_level, (tile_count // group_size,), 0, 4, dtype=jnp.int32)
        levels = jnp.where(jnp.arange(tile_count // group_size, dtype=jnp.int32) == 0, 0, levels)
        in_use = jnp.maximum(jnp.right_shift(jnp.full_like(levels, slot_count), levels), 1)
        in_use = jnp.repeat(in_use, group_size)
    else:
        in_use = jax.random.randint(key_level, (tile_count,), 1, slot_count + 1, dtype=jnp.int32)
        in_use = jnp.where(jnp.arange(tile_count, dtype=jnp.int32) == 0, slot_count, in_use)
    edge_bits = jax.random.randint(key_bits, (tile_count, slot_count, tile_size, tile_size), 0, 8, dtype=jnp.int32) == 0
    full_block = ((jnp.arange(tile_count, dtype=jnp.int32) == 0)[:, None] & (jnp.arange(slot_count, dtype=jnp.int32) == 0)[None, :])[:, :, None, None]
    edge_bits = edge_bits | full_block
    active = (jnp.arange(slot_count, dtype=jnp.int32)[None, :] < in_use[:, None])[:, :, None, None]
    pattern = (edge_bits & active).astype(jnp.int32)
    counts = jnp.sum(pattern, axis=(2, 3)).astype(jnp.int32)
    return (pattern, columns, counts)


def cite_blocks(key):
    return block_draw(key, 11, TILES, K_CITE, CITED // TILE, TILE, T_DEV // TILE, True)


def entity_blocks(key):
    return block_draw(key, 23, TILES, K_ENT, ENTITIES // TILE, TILE, 1, False)


def draw_cite_pattern(key, part):
    return cite_blocks(key)[0]


def draw_cite_tiles(key, part):
    return cite_blocks(key)[1]


def draw_cite_counts(key, part):
    return cite_blocks(key)[2]


def draw_entity_pattern(key, part):
    return entity_blocks(key)[0]


def draw_entity_tiles(key, part):
    return entity_blocks(key)[1]


def draw_entity_counts(key, part):
    return entity_blocks(key)[2]


def touch_ends(entries, stream_key, smallest, top_value):
    shape = entries.shape
    index_at = [jax.random.randint(jax.random.fold_in(stream_key, axis), (), 0, shape[axis]) for axis in range(len(shape))]
    entries = entries.at[tuple(index_at)].set(smallest)
    longest = shape.index(max(shape))
    index_at[longest] = (index_at[longest] + 1) % shape[longest]
    return entries.at[tuple(index_at)].set(top_value)


def block_levels(rng, shape, cuts, smallest, high):
    factor_of = 1.0
    for axis_at, parts in cuts:
        draws = jax.random.uniform(jax.random.fold_in(jax.random.fold_in(rng, 6), axis_at), (parts,), jnp.float32, smallest / len(cuts), high / len(cuts))
        factor_of = factor_of * jnp.repeat(jnp.exp(draws), shape[axis_at] // parts).reshape((-1,) + (1,) * (len(shape) - 1 - axis_at))
    return factor_of


def normal_values(rng, dims, scale, limit, cuts=(), held_as=jnp.bfloat16):
    values = scale * jax.random.normal(rng, dims, jnp.float32)
    if cuts:
        values = values * block_levels(rng, dims, cuts, -0.22, 0.18)
    return jnp.clip(values, -limit, limit).astype(held_as)


def setup_inputs(seed: int = 0) -> dict:
    splits = jax.random.split(jax.random.key(seed), 20)
    papers = normal_values(splits[0], (TARGETS, D), 1.0, 6.0, ((0, 256),))
    cited_rows = normal_values(splits[1], (CITED, D), 1.0, 6.0, ((0, 32),))
    entities = normal_values(splits[2], (ENTITIES, D), 1.0, 6.0, ((0, 8),))
    entity_kinds = touch_ends(jax.random.randint(splits[3], (ENTITIES,), 0, 2), jax.random.fold_in(splits[3], 1), 0, 1).astype(jnp.int32)
    query_weight = normal_values(splits[4], (D, D), D ** -0.5, 0.25)
    key_weight = normal_values(splits[5], (3, D, D), D ** -0.5, 0.25)
    value_weight = normal_values(splits[6], (3, D, D), D ** -0.5, 0.25)
    attention_rel = normal_values(splits[7], (4, HEADS, HEAD_DIM, HEAD_DIM), HEAD_DIM ** -0.5, 0.75)
    message_rel = normal_values(splits[8], (4, HEADS, HEAD_DIM, HEAD_DIM), HEAD_DIM ** -0.5, 0.75)
    relation_prior = jnp.clip(jnp.exp(jax.random.uniform(splits[9], (4, HEADS), jnp.float32, math.log(0.5), math.log(2.5))), 0.5, 2.5)
    output_weight = normal_values(splits[10], (D, D), D ** -0.5, 0.25)
    skip_gate = jnp.clip(jax.random.uniform(splits[11], (1,), jnp.float32, -1.0, 1.0), -1.0, 1.0)
    norm_gain = jnp.clip(1.0 + 0.1 * jax.random.normal(splits[12], (D,), jnp.float32), 0.5, 1.5)
    cite_pattern = draw_cite_pattern(jax.random.fold_in(splits[19], 71), 0)
    cite_tiles = draw_cite_tiles(jax.random.fold_in(splits[19], 71), 0)
    cite_counts = draw_cite_counts(jax.random.fold_in(splits[19], 71), 0)
    entity_pattern = draw_entity_pattern(jax.random.fold_in(splits[19], 71), 0)
    entity_tiles = draw_entity_tiles(jax.random.fold_in(splits[19], 71), 0)
    entity_counts = draw_entity_counts(jax.random.fold_in(splits[19], 71), 0)
    return dict(papers=papers, cited_rows=cited_rows, entities=entities, entity_kinds=entity_kinds, query_weight=query_weight, key_weight=key_weight, value_weight=value_weight, attention_rel=attention_rel, message_rel=message_rel, relation_prior=relation_prior, output_weight=output_weight, skip_gate=skip_gate, norm_gain=norm_gain, cite_pattern=cite_pattern, cite_tiles=cite_tiles, cite_counts=cite_counts, entity_pattern=entity_pattern, entity_tiles=entity_tiles, entity_counts=entity_counts)


CAP = 20.0

def head_split(matrix, head_count):
    return matrix.reshape(matrix.shape[0], head_count, matrix.shape[1] // head_count)

def relate(raw_rows, weight):
    head_count = weight.shape[0]
    mapped = jnp.einsum('nhd,hde->nhe', head_split(raw_rows, head_count).astype(jnp.float32), weight.astype(jnp.float32))
    return mapped.reshape(raw_rows.shape)

def project(source_rows, weight):
    return jnp.dot(source_rows, weight, preferred_element_type=jnp.float32).astype(jnp.bfloat16)

def kind_scales(kind_ids, relation_prior, inv_root):
    author = (kind_ids == 0)[:, None]
    return jnp.where(author, relation_prior[1][None, :], relation_prior[2][None, :]) * inv_root

def entity_side(source_rows, kind_ids, key_weight, value_weight, attention_rel, message_rel):
    author = (kind_ids == 0)[:, None]
    key_raw = jnp.where(author, jnp.dot(source_rows, key_weight[1], preferred_element_type=jnp.float32), jnp.dot(source_rows, key_weight[2], preferred_element_type=jnp.float32)).astype(jnp.bfloat16)
    value_raw = jnp.where(author, jnp.dot(source_rows, value_weight[1], preferred_element_type=jnp.float32), jnp.dot(source_rows, value_weight[2], preferred_element_type=jnp.float32)).astype(jnp.bfloat16)
    key_rows = jnp.where(author, relate(key_raw, attention_rel[1]), relate(key_raw, attention_rel[2])).astype(jnp.bfloat16)
    value_rows = jnp.where(author, relate(value_raw, message_rel[1]), relate(value_raw, message_rel[2])).astype(jnp.bfloat16)
    return (key_rows, value_rows)

def own_term(query_heads, own_key, own_value, scale):
    head_count = query_heads.shape[1]
    own_dot = lax.optimization_barrier(jnp.sum(query_heads.astype(jnp.float32) * head_split(own_key, head_count).astype(jnp.float32), axis=2))
    weights = jnp.exp(CAP * jnp.tanh(own_dot * scale / CAP))
    rounded = lax.optimization_barrier(weights.astype(jnp.bfloat16)).astype(jnp.float32)
    return (rounded[:, :, None] * head_split(own_value, head_count).astype(jnp.float32), weights)

def block_attend(running, query_heads, key_blocks, value_blocks, scales, live_mask):
    head_count = query_heads.shape[1]
    slot_count = key_blocks.shape[0]
    model_width = key_blocks.shape[2]
    key_heads = key_blocks.reshape(slot_count, -1, head_count, model_width // head_count).astype(jnp.float32)
    value_heads = value_blocks.reshape(slot_count, -1, head_count, model_width // head_count).astype(jnp.float32)
    products = jnp.einsum('thd,kshd->khts', query_heads.astype(jnp.float32), key_heads)
    scores = products * jnp.transpose(scales, (0, 2, 1))[:, :, None, :]
    scores = CAP * jnp.tanh(scores / CAP)
    weights = jnp.where(live_mask[:, None, :, :], jnp.exp(scores), 0.0)
    rounded = lax.optimization_barrier(weights.astype(jnp.bfloat16)).astype(jnp.float32)
    numerator, denominator = running
    numerator = numerator + jnp.einsum('khts,kshd->thd', rounded, value_heads)
    denominator = denominator + lax.optimization_barrier(jnp.sum(weights, axis=(0, 3))).T
    return (numerator, denominator)

def finish(numerator, denominator, paper_rows, output_weight, skip_gate, norm_gain):
    mixed = numerator / denominator[:, :, None]
    hidden = jax.nn.gelu(mixed, approximate=False).reshape(paper_rows.shape).astype(jnp.bfloat16)
    projected = jnp.dot(hidden, output_weight, preferred_element_type=jnp.float32)
    alpha = jax.nn.sigmoid(skip_gate[0])
    blended = alpha * projected + (1.0 - alpha) * paper_rows.astype(jnp.float32)
    centre = lax.optimization_barrier(jnp.mean(blended, axis=1, keepdims=True))
    spread = lax.optimization_barrier(jnp.mean(jnp.square(blended - centre), axis=1, keepdims=True))
    return ((blended - centre) * lax.rsqrt(spread + 1e-05) * norm_gain).astype(jnp.bfloat16)

def reference(papers, cited_rows, entities, entity_kinds, query_weight, key_weight, value_weight, attention_rel, message_rel, relation_prior, output_weight, skip_gate, norm_gain, cite_pattern, cite_tiles, cite_counts, entity_pattern, entity_tiles, entity_counts):
    inv_root = 1.0 / math.sqrt(HEAD_DIM)
    queries = project(papers, query_weight)
    own_keys = relate(project(papers, key_weight[0]), attention_rel[3]).astype(jnp.bfloat16)
    own_values = relate(project(papers, value_weight[0]), message_rel[3]).astype(jnp.bfloat16)
    cite_keys = relate(project(cited_rows, key_weight[0]), attention_rel[0]).astype(jnp.bfloat16)
    cite_values = relate(project(cited_rows, value_weight[0]), message_rel[0]).astype(jnp.bfloat16)
    entity_keys, entity_values = entity_side(entities, entity_kinds, key_weight, value_weight, attention_rel, message_rel)
    entity_scales = kind_scales(entity_kinds, relation_prior, inv_root)
    cite_key_blocks = cite_keys.reshape(CITED // TILE, TILE, D)
    cite_value_blocks = cite_values.reshape(CITED // TILE, TILE, D)
    entity_key_blocks = entity_keys.reshape(ENTITIES // TILE, TILE, D)
    entity_value_blocks = entity_values.reshape(ENTITIES // TILE, TILE, D)
    entity_scale_blocks = entity_scales.reshape(ENTITIES // TILE, TILE, HEADS)
    cite_scale = relation_prior[0] * inv_root
    own_scale = relation_prior[3] * inv_root

    def tile_update(position):
        start = (position * TILE).astype(jnp.int32)
        query_heads = head_split(lax.dynamic_slice_in_dim(queries, start, TILE, 0), HEADS)
        own_key = lax.dynamic_slice_in_dim(own_keys, start, TILE, 0)
        own_value = lax.dynamic_slice_in_dim(own_values, start, TILE, 0)
        running = own_term(query_heads, own_key, own_value, own_scale)
        columns = cite_tiles[position]
        live_mask = (cite_pattern[position] > 0) & (cite_counts[position] > 0)[:, None, None]
        scales = jnp.broadcast_to(cite_scale, (K_CITE, TILE, HEADS))
        running = block_attend(running, query_heads, cite_key_blocks[columns], cite_value_blocks[columns], scales, live_mask)
        columns = entity_tiles[position]
        live_mask = (entity_pattern[position] > 0) & (entity_counts[position] > 0)[:, None, None]
        running = block_attend(running, query_heads, entity_key_blocks[columns], entity_value_blocks[columns], entity_scale_blocks[columns], live_mask)
        numerator, denominator = running
        paper_rows = lax.dynamic_slice_in_dim(papers, start, TILE, 0)
        return finish(numerator, denominator, paper_rows, output_weight, skip_gate, norm_gain)
    updated = lax.map(tile_update, jnp.arange(TILES, dtype=jnp.int32))
    return updated.reshape(TARGETS, D)
```

```python
import functools
import math

import jax
import jax.numpy as jnp
from jax import lax
from jax.experimental import pallas as pl
from jax.experimental.pallas import tpu as pltpu
from jax.sharding import PartitionSpec as P

CAP = 20.0
D = 512
HEADS = 8
TILE = 128
PAIRS = 4
F32 = jnp.float32
BF16 = jnp.bfloat16
LOG2E = 1.4426950408889634
ZS, YS, XS = 8, 4, 4
VMEM_LIMIT = 56 * 1024 * 1024


def device_index(x, y, z, core):
    x_hi, x_lo = x // 2, x % 2
    return (x_lo * 16 + z * 2 + core) * 8 + (y * 2 + x_hi)


def permutation(move):
    pairs = []
    for x in range(XS):
        for y in range(YS):
            for z in range(ZS):
                for core in range(2):
                    tx, ty, tz, tc = move(x, y, z, core)
                    pairs.append(
                        (device_index(x, y, z, core), device_index(tx % XS, ty % YS, tz % ZS, tc))
                    )
    return pairs


def send(value, move):
    return lax.ppermute(value, ("paper", "type"), permutation(move))


def core_move(x, y, z, c):
    return (x, y, z, 1 - c)


def z_move(x, y, z, c):
    return (x, y, z + (1 if c == 0 else -1), c)


def x_move(x, y, z, c):
    return (x + (-1 if c == 0 else 1), y, z, c)


def hi_move(x, y, z, c):
    return ({0: 3, 3: 0, 1: 2, 2: 1}[x], y, z, c)


def y_move(step):
    return lambda x, y, z, c: (x, y - step, z, c)


def dot(a, b):
    return lax.dot_general(a, b, (((1,), (0,)), ((), ())), preferred_element_type=F32)


def dot_t(a, b):
    return lax.dot_general(a, b, (((1,), (1,)), ((), ())), preferred_element_type=F32)


def iota(shape, dim):
    return lax.broadcasted_iota(jnp.int32, shape, dim)


def low_half(rows):
    return (iota((rows, TILE), 1) & 64) == 0


def own_kernel(
    papers, query_w, key_w, value_w, att, msg, prior, q2, num0, den0, cite_w, ent_w, blocks, own_w
):
    lane = iota((64, 256), 1)
    row = iota((64, 256), 0)
    for i in range(4):
        place = (lane == row + 64 * i).astype(F32).astype(BF16)
        for t, rel in enumerate((att, msg)):
            for r in range(4):
                for g in range(2):
                    blocks[t, r, g, 64 * i : 64 * i + 64, :] = dot(rel[r, 4 * g + i], place).astype(
                        BF16
                    )
    for t, weight in enumerate((key_w, value_w)):
        for g in range(2):
            cols = slice(256 * g, 256 * g + 256)
            base = weight[0, :, cols]
            own_w[:, 512 * t + 256 * g : 512 * t + 256 * g + 256] = dot(
                base, blocks[t, 3, g]
            ).astype(BF16)
            cite_w[:, 512 * t + 256 * g : 512 * t + 256 * g + 256] = dot(
                base, blocks[t, 0, g]
            ).astype(BF16)
            for u in range(2):
                ent_w[512 * u : 512 * u + 512, 512 * t + 256 * g : 512 * t + 256 * g + 256] = dot(
                    weight[1 + u, :, cols], blocks[t, 1 + u, g]
                ).astype(BF16)
    half = low_half(D)
    zero = jnp.zeros((D, TILE), BF16)
    sums = ((iota((TILE, TILE), 0) & 64) == (iota((TILE, TILE), 1) & 64)).astype(F32).astype(BF16)
    rows = papers[...]
    for j in range(PAIRS):
        cols = slice(TILE * j, TILE * j + TILE)
        q = dot(rows, query_w[:, cols]).astype(BF16)
        k = dot(rows, own_w[:, cols]).astype(BF16)
        v = dot(rows, own_w[:, 512 + TILE * j : 512 + TILE * j + TILE]).astype(BF16)
        q2[0, :, cols] = jnp.where(half, q, zero)
        q2[1, :, cols] = jnp.where(half, zero, q)
        product = q.astype(F32) * k.astype(F32)
        high = product.astype(BF16)
        low = (product - high.astype(F32)).astype(BF16)
        score = dot(high, sums) + dot(low, sums)
        scale = jnp.where(low_half(1), prior[3, 2 * j], prior[3, 2 * j + 1]) * (0.125 / CAP)
        weight = jnp.exp2(jnp.tanh(score * scale) * (CAP * LOG2E))
        den0[:, cols] = weight
        num0[:, cols] = weight.astype(BF16).astype(F32) * v.astype(F32)


def attend_kernel(
    cite_tiles,
    cite_counts,
    entity_tiles,
    entity_counts,
    prior,
    gate,
    part0,
    part1,
    part2,
    part3,
    ent0,
    ent1,
    ent2,
    ent3,
    q2,
    num0,
    den0,
    cite_w,
    ent_w,
    cite_pattern,
    entity_pattern,
    papers,
    output_w,
    gain,
    updated,
    keys,
    values,
    ekeys,
    evalues,
    escale,
    acc,
    slots,
):
    paper_at = lax.axis_index("paper")
    type_at = lax.axis_index("type")
    x_lo, z_at, core = paper_at // 16, (paper_at // 2) % ZS, paper_at % 2
    half = low_half(1)
    one = jnp.ones((1, TILE), BF16)

    def put_values(ref, at, j, v):
        cols = slice(TILE * j, TILE * j + TILE)
        ref[0, at, cols] = jnp.where(half, v, one)
        ref[1, at, cols] = jnp.where(half, one, v)

    for index, part in enumerate((part0, part1, part2, part3)):
        tile_core = core if index % 2 == 0 else 1 - core
        tile_x = x_lo if index < 2 else 1 - x_lo
        step = 2 * tile_core - 1
        order = [(0, 0)] + [(s, o) for s in (1, 2, 3) for o in (0, 1)] + [(4, 0)]
        places = []
        for s, other in order:
            z = (z_at + s * step + ZS) % ZS
            c = tile_core if other == 0 else 1 - tile_core
            places.append(pl.multiple_of((tile_x * 16 + z * 2 + c) * TILE, TILE))
        rows = part[...]
        for n in range(4):
            made = dot(rows, cite_w[:, 256 * n : 256 * n + 256]).astype(BF16)
            for t in range(8):
                at = pl.ds(places[t], TILE)
                block = made[TILE * t : TILE * t + TILE]
                if n < 2:
                    keys[at, 256 * n : 256 * n + 256] = block
                else:
                    put_values(values, at, 2 * (n - 2), block[:, :TILE])
                    put_values(values, at, 2 * (n - 2) + 1, block[:, TILE:])
    y_at, hi_at = type_at // 2, type_at % 2
    pick = (iota((8, TILE), 1) == 0).astype(F32).astype(BF16)
    for s, part in enumerate((ent0, ent1, ent2, ent3)):
        places = []
        for other in range(2):
            y = (y_at + (0, 1, 3, 2)[s]) % YS
            hi = hi_at if other == 0 else 1 - hi_at
            places.append(y * 2 + hi)
        rows = part[:, :D]
        kind = part[:, D : D + TILE]
        kind4 = jnp.concatenate([kind] * 4, axis=1)
        split = jnp.concatenate([rows * (1 - kind4), rows * kind4], axis=1)
        for n in range(4):
            made = dot(split, ent_w[:, 256 * n : 256 * n + 256]).astype(BF16)
            for t in range(2):
                at = pl.ds(pl.multiple_of(places[t] * TILE, TILE), TILE)
                block = made[TILE * t : TILE * t + TILE]
                if n < 2:
                    ekeys[at, 256 * n : 256 * n + 256] = block
                else:
                    put_values(evalues, at, 2 * (n - 2), block[:, :TILE])
                    put_values(evalues, at, 2 * (n - 2) + 1, block[:, TILE:])
        for t in range(2):
            kind_row = dot_t(pick, kind[TILE * t : TILE * t + TILE])[0:1]
            for h in range(HEADS):
                escale[places[t], h : h + 1, :] = jnp.where(
                    kind_row < 0.5, prior[1, h], prior[2, h]
                ) * (0.125 / CAP)

    alpha = jax.nn.sigmoid(jnp.full((1, D), gate[0], F32))

    def tile_body(a, carry):
        rows = pl.ds(pl.multiple_of(a * TILE, TILE), TILE)
        count = jnp.int32(0)
        for k in range(8):
            slots[count] = k
            count = count + (cite_counts[a, k] > 0).astype(jnp.int32)

        def block_pair(src_k, src_v, t0, t1, mask, scale_of, first):
            at0 = pl.ds(pl.multiple_of(t0 * TILE, TILE), TILE)
            at1 = pl.ds(pl.multiple_of(t1 * TILE, TILE), TILE)
            for j in range(PAIRS):
                cols = slice(TILE * j, TILE * j + TILE)
                kk = jnp.concatenate([src_k[at0, cols], src_k[at1, cols]], axis=0)
                for e in range(2):
                    vv = jnp.concatenate([src_v[e, at0, cols], src_v[e, at1, cols]], axis=0)
                    score = dot_t(q2[e, rows, cols], kk)
                    weight = jnp.exp2(jnp.tanh(score * scale_of(2 * j + e)) * (CAP * LOG2E))
                    weight = weight.astype(BF16) * mask
                    got = dot(weight, vv)
                    if first:
                        acc[e, rows, cols] = got
                    else:
                        acc[e, rows, cols] += got

        def mask_of(pattern, k, live):
            return jnp.where((pattern[a, k] > 0) & live, 1.0, 0.0).astype(BF16)

        e0, e1 = entity_tiles[a, 0], entity_tiles[a, 1]
        mask = jnp.concatenate(
            [mask_of(entity_pattern, k, entity_counts[a, k] > 0) for k in range(2)], axis=1
        )
        block_pair(
            ekeys,
            evalues,
            e0,
            e1,
            mask,
            lambda h: jnp.concatenate([escale[e0, h : h + 1, :], escale[e1, h : h + 1, :]], axis=1),
            True,
        )

        def pair_body(i, carry):
            k0 = slots[2 * i]
            second = 2 * i + 1 < count
            k1 = jnp.where(second, slots[2 * i + 1], k0)
            mask = jnp.concatenate(
                [mask_of(cite_pattern, k0, True), mask_of(cite_pattern, k1, second)], axis=1
            )
            block_pair(
                keys,
                values,
                cite_tiles[a, k0],
                cite_tiles[a, k1],
                mask,
                lambda h: prior[0, h] * (0.125 / CAP),
                False,
            )
            return carry

        lax.fori_loop(0, (count + 1) // 2, pair_body, 0)

        hidden = []
        for j in range(PAIRS):
            cols = slice(TILE * j, TILE * j + TILE)
            even, odd = acc[0, rows, cols], acc[1, rows, cols]
            num = jnp.where(half, even, odd) + num0[rows, cols]
            den = pltpu.roll(jnp.where(half, odd, even), 64, 1) + den0[rows, cols]
            mixed = num / den
            hidden.append((0.5 * mixed * (1.0 + lax.erf(mixed * math.sqrt(0.5)))).astype(BF16))
        projected = dot(jnp.concatenate(hidden, axis=1), output_w[...])
        blended = alpha * projected + (1.0 - alpha) * papers[rows, :].astype(F32)
        centre = jnp.mean(blended, axis=1, keepdims=True)
        blended = blended - centre
        spread = jnp.mean(jnp.square(blended), axis=1, keepdims=True)
        updated[rows, :] = (blended * lax.rsqrt(spread + 1e-05) * gain[...]).astype(BF16)
        return carry

    lax.fori_loop(0, 4, tile_body, 0)


def per_device(
    papers,
    cited_rows,
    entities,
    entity_kinds,
    query_weight,
    key_weight,
    value_weight,
    attention_rel,
    message_rel,
    relation_prior,
    output_weight,
    skip_gate,
    norm_gain,
    cite_pattern,
    cite_tiles,
    cite_counts,
    entity_pattern,
    entity_tiles,
    entity_counts,
):
    vmem = pl.BlockSpec(memory_space=pltpu.VMEM)
    smem = pl.BlockSpec(memory_space=pltpu.SMEM)
    shape = jax.ShapeDtypeStruct

    pair = jnp.concatenate([cited_rows, send(cited_rows, core_move)], axis=0)
    kinds = jnp.broadcast_to(entity_kinds.astype(BF16)[:, None], (TILE, TILE))
    ent_own = jnp.concatenate([entities, kinds], axis=1)
    ent_pair = jnp.concatenate([ent_own, send(ent_own, hi_move)], axis=0)
    z1 = send(pair, z_move)
    ent1 = send(ent_pair, y_move(1))
    ent3 = send(ent_pair, y_move(3))
    z2 = send(z1, z_move)
    ent2 = send(ent_pair, y_move(2))
    z3 = send(z2, z_move)
    z4 = send(z3[:TILE], z_move)
    part0 = jnp.concatenate([cited_rows, z1, z2, z3, z4], axis=0)
    part2 = send(part0, x_move)
    part1 = send(part0, core_move)
    part3 = send(part2, core_move)

    q2, num0, den0, cite_w, ent_w = pl.pallas_call(
        own_kernel,
        out_shape=(
            shape((2, 512, D), BF16),
            shape((512, D), F32),
            shape((512, D), F32),
            shape((D, 2 * D), BF16),
            shape((2 * D, 2 * D), BF16),
        ),
        in_specs=[vmem] * 6 + [smem],
        out_specs=(vmem,) * 5,
        scratch_shapes=[
            pltpu.VMEM((2, 4, 2, 256, 256), BF16),
            pltpu.VMEM((D, 2 * D), BF16),
        ],
        compiler_params=pltpu.CompilerParams(vmem_limit_bytes=VMEM_LIMIT),
        cost_estimate=pl.CostEstimate(flops=4 * 10**9, bytes_accessed=10 * 2**20, transcendentals=0),
        name="own_terms",
    )(papers, query_weight, key_weight, value_weight, attention_rel, message_rel, relation_prior)

    return pl.pallas_call(
        attend_kernel,
        out_shape=shape((512, D), BF16),
        in_specs=[smem] * 6 + [vmem] * 18,
        out_specs=vmem,
        scratch_shapes=[
            pltpu.VMEM((4096, D), BF16),
            pltpu.VMEM((2, 4096, D), BF16),
            pltpu.VMEM((1024, D), BF16),
            pltpu.VMEM((2, 1024, D), BF16),
            pltpu.VMEM((8, HEADS, TILE), F32),
            pltpu.VMEM((2, 512, D), F32),
            pltpu.SMEM((16,), jnp.int32),
        ],
        compiler_params=pltpu.CompilerParams(vmem_limit_bytes=VMEM_LIMIT),
        cost_estimate=pl.CostEstimate(flops=10**10, bytes_accessed=20 * 2**20, transcendentals=10**7),
        name="attend_and_finish",
    )(
        cite_tiles,
        cite_counts,
        entity_tiles,
        entity_counts,
        relation_prior,
        skip_gate,
        part0,
        part1,
        part2,
        part3,
        ent_pair,
        ent1,
        ent3,
        ent2,
        q2,
        num0,
        den0,
        cite_w,
        ent_w,
        cite_pattern,
        entity_pattern,
        papers,
        output_weight,
        norm_gain.reshape(1, D),
    )


def solution(mesh):
    split = P(("paper", "type"))
    in_specs = (
        P(("paper", "type"), None),
        P("paper", None),
        P("type", None),
        P("type"),
        P(),
        P(),
        P(),
        P(),
        P(),
        P(),
        P(),
        P(),
        P(),
        split,
        split,
        split,
        split,
        split,
        split,
    )
    return jax.shard_map(
        per_device, mesh=mesh, in_specs=in_specs, out_specs=P(("paper", "type"), None), check_vma=False
    )
```

```python
import functools
import math

import jax
import jax.numpy as jnp
from jax import lax
from jax.experimental import pallas as pl
from jax.experimental.pallas import tpu as pltpu
from jax.sharding import PartitionSpec as P

CAP = 20.0
D = 512
HEADS = 8
TILE = 128
PAIRS = 4
F32 = jnp.float32
BF16 = jnp.bfloat16
LOG2E = 1.4426950408889634
ZS, YS, XS = 8, 4, 4


def device_index(x, y, z, core):
    x_hi, x_lo = x // 2, x % 2
    return (x_lo * 16 + z * 2 + core) * 8 + (y * 2 + x_hi)


def permutation(move):
    pairs = []
    for x in range(XS):
        for y in range(YS):
            for z in range(ZS):
                for core in range(2):
                    tx, ty, tz, tc = move(x, y, z, core)
                    pairs.append(
                        (device_index(x, y, z, core), device_index(tx % XS, ty % YS, tz % ZS, tc))
                    )
    return pairs


def send(value, move):
    return lax.ppermute(value, ("paper", "type"), permutation(move))


def core_move(x, y, z, c):
    return (x, y, z, 1 - c)


def x_up(x, y, z, c):
    return (x - 1, y, z, c)


def x_down(x, y, z, c):
    return (x + 1, y, z, c)


def hi_move(x, y, z, c):
    return ({0: 3, 3: 0, 1: 2, 2: 1}[x], y, z, c)


def dot(a, b):
    return lax.dot_general(a, b, (((1,), (0,)), ((), ())), preferred_element_type=F32)


def dot_t(a, b):
    return lax.dot_general(a, b, (((1,), (1,)), ((), ())), preferred_element_type=F32)


def iota(shape, dim):
    return lax.broadcasted_iota(jnp.int32, shape, dim)


def low_half(rows):
    return (iota((rows, TILE), 1) & 64) == 0


def head_scale(prior, relation, j):
    return jnp.where(low_half(1), prior[relation, 2 * j], prior[relation, 2 * j + 1]) * (0.125 / CAP)


def mask_of(pattern, a, k, live):
    return jnp.where((pattern[a, k] > 0) & live, 1.0, 0.0).astype(BF16)


def fold_kernel(key_w, value_w, att, msg, cite_w, own_w, ent_w, blocks):
    lane = iota((64, 256), 1)
    row = iota((64, 256), 0)
    for i in range(4):
        place = (lane == row + 64 * i).astype(F32).astype(BF16)
        for t, rel in enumerate((att, msg)):
            for r in range(4):
                for g in range(2):
                    blocks[t, r, g, 64 * i : 64 * i + 64, :] = dot(rel[r, 4 * g + i], place).astype(
                        BF16
                    )
    for t, weight in enumerate((key_w, value_w)):
        for g in range(2):
            cols = slice(256 * g, 256 * g + 256)
            base = weight[0, :, cols]
            to = slice(512 * t + 256 * g, 512 * t + 256 * g + 256)
            cite_w[:, to] = dot(base, blocks[t, 0, g]).astype(BF16)
            own_w[:, to] = dot(base, blocks[t, 3, g]).astype(BF16)
            for u in range(2):
                ent_w[512 * u : 512 * u + 512, to] = dot(
                    weight[1 + u, :, cols], blocks[t, 1 + u, g]
                ).astype(BF16)


def own_kernel(papers, query_w, own_w, prior, q2, acc):
    half = low_half(1)
    zero = jnp.zeros((1, TILE), BF16)
    sums = ((iota((TILE, TILE), 0) & 64) == (iota((TILE, TILE), 1) & 64)).astype(F32).astype(BF16)
    rows = papers[...]
    for g in range(2):
        cols = slice(256 * g, 256 * g + 256)
        q_pairs = dot(rows, query_w[:, cols]).astype(BF16)
        k_pairs = dot(rows, own_w[:, cols]).astype(BF16)
        v_pairs = dot(rows, own_w[:, 512 + 256 * g : 512 + 256 * g + 256]).astype(BF16)
        for i in range(2):
            j = 2 * g + i
            part = slice(TILE * i, TILE * i + TILE)
            q, k, v = q_pairs[:, part], k_pairs[:, part], v_pairs[:, part]
            cols = slice(TILE * j, TILE * j + TILE)
            q2[0, :, cols] = jnp.where(half, q, zero)
            q2[1, :, cols] = jnp.where(half, zero, q)
            product = q.astype(F32) * k.astype(F32)
            high = product.astype(BF16)
            low = (product - high.astype(F32)).astype(BF16)
            score = dot(high, sums) + dot(low, sums)
            weight = jnp.exp2(jnp.tanh(score * head_scale(prior, 3, j)) * (CAP * LOG2E))
            den = pltpu.roll(weight, 64, 1)
            num = weight.astype(BF16).astype(F32) * v.astype(F32)
            acc[0, :, cols] = jnp.where(half, num, den)
            acc[1, :, cols] = jnp.where(half, den, num)


def source_kernel(part0, part1, part2, cite_w, pairs):
    base = 0
    for part in (part0, part1, part2):
        rows = part[...]
        at = slice(base, base + rows.shape[0])
        for n in range(4):
            pairs[at, 256 * n : 256 * n + 256] = dot(rows, cite_w[:, 256 * n : 256 * n + 256]).astype(
                BF16
            )
        base += rows.shape[0]


def entity_kernel(prior, ent0, ent1, ent_w, pairs, scales):
    type_at = lax.axis_index("type")
    y_at, hi_at = type_at // 2, type_at % 2
    pick = (iota((8, TILE), 1) == 0).astype(F32).astype(BF16)
    for s, part in enumerate((ent0, ent1)):
        rows = part[:, :D]
        kind = part[:, D : D + TILE]
        kind4 = jnp.concatenate([kind] * 4, axis=1)
        split = jnp.concatenate([rows * (1 - kind4), rows * kind4], axis=1)
        places = []
        for i in range(4):
            y = y_at if s == 0 else 3 - y_at
            y = y if i < 2 else y + 1 - 2 * (y % 2)
            places.append(y * 2 + (hi_at if i % 2 == 0 else 1 - hi_at))
        for n in range(4):
            made = dot(split, ent_w[:, 256 * n : 256 * n + 256]).astype(BF16)
            for t in range(4):
                at = pl.ds(pl.multiple_of(places[t] * TILE, TILE), TILE)
                pairs[at, 256 * n : 256 * n + 256] = made[TILE * t : TILE * t + TILE]
        for t in range(4):
            kind_row = dot_t(pick, kind[TILE * t : TILE * t + TILE])[0:1]
            for h in range(HEADS):
                scales[places[t], h : h + 1, :] = jnp.where(
                    kind_row < 0.5, prior[1, h], prior[2, h]
                ) * (0.125 / CAP)


def block_pair(q2, acc, rows, pairs, at0, at1, mask, scale_of):
    half = low_half(1)
    one = jnp.ones((1, TILE), BF16)
    at0 = pl.ds(pl.multiple_of(at0, TILE), TILE)
    at1 = pl.ds(pl.multiple_of(at1, TILE), TILE)
    for j in range(PAIRS):
        cols = slice(TILE * j, TILE * j + TILE)
        to = slice(D + TILE * j, D + TILE * j + TILE)
        kk = jnp.concatenate([pairs[at0, cols], pairs[at1, cols]], axis=0)
        vv = jnp.concatenate([pairs[at0, to], pairs[at1, to]], axis=0)
        for e in range(2):
            score = dot_t(q2[e, rows, cols], kk)
            weight = jnp.exp2(jnp.tanh(score * scale_of(2 * j + e)) * (CAP * LOG2E))
            value = jnp.where(half, vv, one) if e == 0 else jnp.where(half, one, vv)
            acc[e, rows, cols] += dot(weight.astype(BF16) * mask, value)


def final_kernel(
    tiles,
    counts,
    entity_tiles,
    entity_counts,
    prior,
    gate,
    near,
    near_other,
    far,
    far_other,
    entity_in,
    scales,
    q2_in,
    acc_in,
    pattern_in,
    entity_pattern_in,
    papers_in,
    output_w_in,
    gain,
    updated,
    pairs,
    entity_pairs,
    q2,
    acc,
    pattern,
    entity_pattern,
    papers,
    output_w,
    slots,
    sems,
):
    copies = []
    for source, target in (
        (q2_in, q2),
        (acc_in, acc),
        (entity_pattern_in, entity_pattern),
        (entity_in, entity_pairs),
        (near, pairs.at[pl.ds(0, 1024)]),
        (near_other, pairs.at[pl.ds(1024, 1024)]),
        (far, pairs.at[pl.ds(2048, 1024)]),
        (far_other, pairs.at[pl.ds(3072, 1024)]),
        (pattern_in, pattern),
        (output_w_in, output_w),
        (papers_in, papers),
    ):
        made = pltpu.make_async_copy(source, target, sems.at[len(copies)])
        made.start()
        copies.append(made)
    paper_at = lax.axis_index("paper")
    x_lo, z_at, core = paper_at // 16, (paper_at // 2) % ZS, paper_at % 2
    half = low_half(1)
    alpha = jax.nn.sigmoid(jnp.full((1, D), gate[0], F32))
    for made in copies:
        made.wait()

    def place(tile):
        far = jnp.where(tile // 16 == x_lo, 0, 2048)
        other = jnp.where(tile % 2 == core, 0, 1024)
        ahead = ((tile // 2) % ZS + ZS - z_at) % ZS
        at = jnp.where(ahead > 4, 2 * (ZS - ahead), jnp.maximum(2 * ahead - 1, 0))
        return far + other + at * TILE

    def tile_body(a, carry):
        rows = pl.ds(pl.multiple_of(a * TILE, TILE), TILE)
        e0, e1 = entity_tiles[a, 0], entity_tiles[a, 1]
        mask = jnp.concatenate(
            [mask_of(entity_pattern, a, k, entity_counts[a, k] > 0) for k in range(2)], axis=1
        )
        block_pair(
            q2,
            acc,
            rows,
            entity_pairs,
            e0 * TILE,
            e1 * TILE,
            mask,
            lambda h: jnp.concatenate([scales[e0, h : h + 1, :], scales[e1, h : h + 1, :]], axis=1),
        )
        count = jnp.int32(0)
        for k in range(8):
            slots[count] = k
            count = count + (counts[a, k] > 0).astype(jnp.int32)

        def pair_body(i, carry):
            k0 = slots[2 * i]
            second = 2 * i + 1 < count
            k1 = jnp.where(second, slots[2 * i + 1], k0)
            mask = jnp.concatenate(
                [mask_of(pattern, a, k0, True), mask_of(pattern, a, k1, second)], axis=1
            )
            block_pair(
                q2,
                acc,
                rows,
                pairs,
                place(tiles[a, k0]),
                place(tiles[a, k1]),
                mask,
                lambda h: prior[0, h] * (0.125 / CAP),
            )
            return carry

        lax.fori_loop(0, (count + 1) // 2, pair_body, 0)

        hidden = []
        for j in range(PAIRS):
            cols = slice(TILE * j, TILE * j + TILE)
            even, odd = acc[0, rows, cols], acc[1, rows, cols]
            num = jnp.where(half, even, odd)
            den = pltpu.roll(jnp.where(half, odd, even), 64, 1)
            mixed = num / den
            hidden.append((0.5 * mixed * (1.0 + lax.erf(mixed * math.sqrt(0.5)))).astype(BF16))
        projected = dot(jnp.concatenate(hidden, axis=1), output_w[...])
        blended = alpha * projected + (1.0 - alpha) * papers[rows, :].astype(F32)
        centre = jnp.mean(blended, axis=1, keepdims=True)
        blended = blended - centre
        spread = jnp.mean(jnp.square(blended), axis=1, keepdims=True)
        updated[rows, :] = (blended * lax.rsqrt(spread + 1e-05) * gain[...]).astype(BF16)
        return carry

    lax.fori_loop(0, 4, tile_body, 0)


def per_device(
    papers,
    cited_rows,
    entities,
    entity_kinds,
    query_weight,
    key_weight,
    value_weight,
    attention_rel,
    message_rel,
    relation_prior,
    output_weight,
    skip_gate,
    norm_gain,
    cite_pattern,
    cite_tiles,
    cite_counts,
    entity_pattern,
    entity_tiles,
    entity_counts,
):
    vmem = pl.BlockSpec(memory_space=pltpu.VMEM)
    smem = pl.BlockSpec(memory_space=pltpu.SMEM)
    shape = jax.ShapeDtypeStruct
    tie = lax.optimization_barrier

    def call(kernel, outs, ins, mib, flops, name, scratch=()):
        return pl.pallas_call(
            kernel,
            out_shape=outs,
            in_specs=ins,
            out_specs=jax.tree.map(lambda _: vmem, outs),
            scratch_shapes=scratch,
            compiler_params=pltpu.CompilerParams(vmem_limit_bytes=mib * 2**20),
            cost_estimate=pl.CostEstimate(
                flops=flops * 10**9, bytes_accessed=8 * 2**20, transcendentals=0
            ),
            name=name,
        )

    def up(value):
        return send(value, lambda x, y, z, c: (x, y, z + 1, c))

    def down(value):
        return send(value, lambda x, y, z, c: (x, y, z - 1, c))

    kinds = jnp.broadcast_to(entity_kinds.astype(BF16)[:, None], (TILE, TILE))
    ent_own = jnp.concatenate([entities, kinds], axis=1)
    a1, b1 = down(cited_rows), up(cited_rows)
    ent_x = send(ent_own, hi_move)
    a1, b1, ent_x = tie((a1, b1, ent_x))
    ent_pair = jnp.concatenate([ent_own, ent_x], axis=0)
    a2, b2 = down(a1), up(b1)
    ent_y = send(ent_pair, lambda x, y, z, c: (x, y ^ 1, z, c))
    a2, b2, ent_y = tie((a2, b2, ent_y))
    first = jnp.concatenate([cited_rows, a1, b1, a2], axis=0)
    ent_four = jnp.concatenate([ent_pair, ent_y], axis=0)
    a3, b3 = down(a2), up(b2)
    far_first = send(first, x_up)
    ent_rest = send(ent_four, lambda x, y, z, c: (x, 3 - y, z, c))
    cite_w, own_w, ent_w = call(
        fold_kernel,
        (shape((D, 2 * D), BF16), shape((D, 2 * D), BF16), shape((2 * D, 2 * D), BF16)),
        [vmem] * 4,
        20,
        3,
        "fold_maps",
        [pltpu.VMEM((2, 4, 2, 256, 256), BF16)],
    )(key_weight, value_weight, attention_rel, message_rel)
    a3, b3, cite_w = tie((a3, b3, cite_w))
    a4 = down(a3)
    second = jnp.concatenate([b2, a3], axis=0)
    far_second = send(second, x_up)
    a4, second = tie((a4, second))
    third = jnp.concatenate([b3, a4], axis=0)
    far_third = send(third, x_down)
    source = call(source_kernel, shape((1024, 2 * D), BF16), [vmem] * 4, 16, 2, "cited_sources")
    near = source(first, second, third, cite_w)
    near_other = send(near, core_move)
    entity_pairs, scales = call(
        entity_kernel,
        (shape((1024, 2 * D), BF16), shape((8, HEADS, TILE), F32)),
        [smem] + [vmem] * 3,
        20,
        2,
        "entity_sources",
    )(relation_prior, ent_four, ent_rest, ent_w)
    far_first, far_second, far_third, entity_pairs = tie(
        (far_first, far_second, far_third, entity_pairs)
    )
    far = source(far_first, far_second, far_third, cite_w)
    far_other = send(far, core_move)
    far, own_w = tie((far, own_w))
    q2, acc = call(
        own_kernel,
        (shape((2, 512, D), BF16), shape((2, 512, D), F32)),
        [vmem] * 3 + [smem],
        16,
        1,
        "own_terms",
    )(papers, query_weight, own_w, relation_prior)

    hbm = pl.BlockSpec(memory_space=pl.ANY)
    return call(
        final_kernel,
        shape((512, D), BF16),
        [smem] * 6 + [hbm] * 5 + [vmem] + [hbm] * 6 + [vmem],
        26,
        4,
        "attend_and_finish",
        [
            pltpu.VMEM((4096, 2 * D), BF16),
            pltpu.VMEM((1024, 2 * D), BF16),
            pltpu.VMEM((2, 512, D), BF16),
            pltpu.VMEM((2, 512, D), F32),
            pltpu.VMEM((4, 8, TILE, TILE), jnp.int32),
            pltpu.VMEM((4, 2, TILE, TILE), jnp.int32),
            pltpu.VMEM((512, D), BF16),
            pltpu.VMEM((D, D), BF16),
            pltpu.SMEM((16,), jnp.int32),
            pltpu.SemaphoreType.DMA((11,)),
        ],
    )(
        cite_tiles,
        cite_counts,
        entity_tiles,
        entity_counts,
        relation_prior,
        skip_gate,
        near,
        near_other,
        far,
        far_other,
        entity_pairs,
        scales,
        q2,
        acc,
        cite_pattern,
        entity_pattern,
        papers,
        output_weight,
        norm_gain.reshape(1, D),
    )


def solution(mesh):
    split = P(("paper", "type"))
    in_specs = (
        P(("paper", "type"), None),
        P("paper", None),
        P("type", None),
        P("type"),
        P(),
        P(),
        P(),
        P(),
        P(),
        P(),
        P(),
        P(),
        P(),
        split,
        split,
        split,
        split,
        split,
        split,
    )
    return jax.shard_map(
        per_device, mesh=mesh, in_specs=in_specs, out_specs=P(("paper", "type"), None), check_vma=False
    )
```

```python
import functools
import math

import jax
import jax.numpy as jnp
from jax import lax
from jax.experimental import pallas as pl
from jax.experimental.pallas import tpu as pltpu
from jax.sharding import PartitionSpec as P

CAP = 20.0
D = 512
HEADS = 8
TILE = 128
PAIRS = 4
F32 = jnp.float32
BF16 = jnp.bfloat16
LOG2E = 1.4426950408889634
ZS, YS, XS = 8, 4, 4
FINAL_MIB = 34


def device_index(x, y, z, core):
    x_hi, x_lo = x // 2, x % 2
    return (x_lo * 16 + z * 2 + core) * 8 + (y * 2 + x_hi)


def permutation(move):
    pairs = []
    for x in range(XS):
        for y in range(YS):
            for z in range(ZS):
                for core in range(2):
                    tx, ty, tz, tc = move(x, y, z, core)
                    pairs.append(
                        (device_index(x, y, z, core), device_index(tx % XS, ty % YS, tz % ZS, tc))
                    )
    return pairs


def send(value, move):
    return lax.ppermute(value, ("paper", "type"), permutation(move))


def core_move(x, y, z, c):
    return (x, y, z, 1 - c)


def x_up(x, y, z, c):
    return (x - 1, y, z, c)


def x_down(x, y, z, c):
    return (x + 1, y, z, c)


def hi_move(x, y, z, c):
    return ({0: 3, 3: 0, 1: 2, 2: 1}[x], y, z, c)


def dot(a, b):
    return lax.dot_general(a, b, (((1,), (0,)), ((), ())), preferred_element_type=F32)


def dot_t(a, b):
    return lax.dot_general(a, b, (((1,), (1,)), ((), ())), preferred_element_type=F32)


def iota(shape, dim):
    return lax.broadcasted_iota(jnp.int32, shape, dim)


def low_half(rows):
    return (iota((rows, TILE), 1) & 64) == 0


def head_scale(prior, relation, j):
    return jnp.where(low_half(1), prior[relation, 2 * j], prior[relation, 2 * j + 1]) * (0.125 / CAP)


def mask_of(pattern, a, k, live):
    return jnp.where((pattern[a, k] > 0) & live, 1.0, 0.0).astype(BF16)


def fold_kernel(key_w, value_w, att, msg, cite_w, own_w, ent_w, blocks):
    lane = iota((64, 256), 1)
    row = iota((64, 256), 0)
    for i in range(4):
        place = (lane == row + 64 * i).astype(F32).astype(BF16)
        for t, rel in enumerate((att, msg)):
            for r in range(4):
                for g in range(2):
                    blocks[t, r, g, 64 * i : 64 * i + 64, :] = dot(rel[r, 4 * g + i], place).astype(
                        BF16
                    )
    for t, weight in enumerate((key_w, value_w)):
        for g in range(2):
            cols = slice(256 * g, 256 * g + 256)
            base = weight[0, :, cols]
            to = slice(512 * t + 256 * g, 512 * t + 256 * g + 256)
            cite_w[:, to] = dot(base, blocks[t, 0, g]).astype(BF16)
            own_w[:, to] = dot(base, blocks[t, 3, g]).astype(BF16)
            for u in range(2):
                ent_w[512 * u : 512 * u + 512, to] = dot(
                    weight[1 + u, :, cols], blocks[t, 1 + u, g]
                ).astype(BF16)


def own_kernel(papers, query_w, own_w, prior, q2, acc):
    half = low_half(1)
    zero = jnp.zeros((1, TILE), BF16)
    sums = ((iota((TILE, TILE), 0) & 64) == (iota((TILE, TILE), 1) & 64)).astype(F32).astype(BF16)
    rows = papers[...]
    for g in range(2):
        cols = slice(256 * g, 256 * g + 256)
        q_pairs = dot(rows, query_w[:, cols]).astype(BF16)
        k_pairs = dot(rows, own_w[:, cols]).astype(BF16)
        v_pairs = dot(rows, own_w[:, 512 + 256 * g : 512 + 256 * g + 256]).astype(BF16)
        for i in range(2):
            j = 2 * g + i
            part = slice(TILE * i, TILE * i + TILE)
            q, k, v = q_pairs[:, part], k_pairs[:, part], v_pairs[:, part]
            cols = slice(TILE * j, TILE * j + TILE)
            q2[0, :, cols] = jnp.where(half, q, zero)
            q2[1, :, cols] = jnp.where(half, zero, q)
            product = q.astype(F32) * k.astype(F32)
            high = product.astype(BF16)
            low = (product - high.astype(F32)).astype(BF16)
            score = dot(high, sums) + dot(low, sums)
            weight = jnp.exp2(jnp.tanh(score * head_scale(prior, 3, j)) * (CAP * LOG2E))
            acc[0, :, cols] = weight.astype(BF16).astype(F32) * v.astype(F32)
            acc[1, :, cols] = weight


def source_kernel(part0, part1, part2, cite_w, pairs):
    base = 0
    for part in (part0, part1, part2):
        rows = part[...]
        at = slice(base, base + rows.shape[0])
        for n in range(4):
            pairs[at, 256 * n : 256 * n + 256] = dot(rows, cite_w[:, 256 * n : 256 * n + 256]).astype(
                BF16
            )
        base += rows.shape[0]


def entity_kernel(prior, ent0, ent1, ent_w, pairs, scales):
    type_at = lax.axis_index("type")
    y_at, hi_at = type_at // 2, type_at % 2
    pick = (iota((8, TILE), 1) == 0).astype(F32).astype(BF16)
    for s, part in enumerate((ent0, ent1)):
        rows = part[:, :D]
        kind = part[:, D : D + TILE]
        kind4 = jnp.concatenate([kind] * 4, axis=1)
        split = jnp.concatenate([rows * (1 - kind4), rows * kind4], axis=1)
        places = []
        for i in range(4):
            y = y_at if s == 0 else 3 - y_at
            y = y if i < 2 else y + 1 - 2 * (y % 2)
            places.append(y * 2 + (hi_at if i % 2 == 0 else 1 - hi_at))
        for n in range(4):
            made = dot(split, ent_w[:, 256 * n : 256 * n + 256]).astype(BF16)
            for t in range(4):
                at = pl.ds(pl.multiple_of(places[t] * TILE, TILE), TILE)
                pairs[at, 256 * n : 256 * n + 256] = made[TILE * t : TILE * t + TILE]
        for t in range(4):
            kind_row = dot_t(pick, kind[TILE * t : TILE * t + TILE])[0:1]
            for h in range(HEADS):
                scales[places[t], h : h + 1, :] = jnp.where(
                    kind_row < 0.5, prior[1, h], prior[2, h]
                ) * (0.125 / CAP)


def final_kernel(
    tiles,
    counts,
    entity_tiles,
    entity_counts,
    prior,
    gate,
    near,
    near_other,
    far,
    far_other,
    entity_in,
    scales,
    q2,
    acc,
    pattern,
    entity_pattern,
    papers,
    output_w,
    gain,
    updated,
    pairs,
    hidden,
    sems,
):
    copies = []
    for at, source in enumerate((entity_in, near, near_other, far, far_other)):
        to = pl.ds(4096, 1024) if at == 0 else pl.ds(1024 * (at - 1), 1024)
        made = pltpu.make_async_copy(source, pairs.at[to], sems.at[at])
        made.start()
        copies.append(made)
    paper_at = lax.axis_index("paper")
    x_lo, z_at, core = paper_at // 16, (paper_at // 2) % ZS, paper_at % 2
    half = low_half(1)
    alpha = jax.nn.sigmoid(jnp.full((1, D), gate[0], F32))

    def place(tile):
        far = jnp.where(tile // 16 == x_lo, 0, 2048)
        other = jnp.where(tile % 2 == core, 0, 1024)
        ahead = ((tile // 2) % ZS + ZS - z_at) % ZS
        at = jnp.where(ahead > 4, 2 * (ZS - ahead), jnp.maximum(2 * ahead - 1, 0))
        return far + other + at * TILE

    for made in copies:
        made.wait()

    def tile_block(a, width):
        rows = pl.ds(pl.multiple_of(a * TILE, TILE), TILE)
        nodes = [entity_tiles[k, a] for k in range(2)]
        starts = [place(tiles[a, k]) for k in range(width)] + [4096 + n * TILE for n in nodes]
        places = [pl.ds(pl.multiple_of(at, TILE), TILE) for at in starts]
        mask = jnp.concatenate(
            [mask_of(pattern, a, k, counts[a, k] > 0) for k in range(width)]
            + [mask_of(entity_pattern, a, k, entity_counts[k, a] > 0) for k in range(2)],
            axis=1,
        )

        def scores(j):
            cols = slice(TILE * j, TILE * j + TILE)
            keys = jnp.concatenate([pairs[at, cols] for at in places], axis=0)
            both = jnp.concatenate([q2[0, rows, cols], q2[1, rows, cols]], axis=0)
            return dot_t(both, keys)

        def weights(score, h):
            scale = jnp.concatenate(
                [jnp.full((1, width * TILE), prior[0, h] * (0.125 / CAP), F32)]
                + [scales[n, h : h + 1, :] for n in nodes],
                axis=1,
            )
            return jnp.exp2(jnp.tanh(score * scale) * (CAP * LOG2E)).astype(BF16) * mask

        score = scores(0)
        for j in range(PAIRS):
            ahead = scores(j + 1) if j + 1 < PAIRS else None
            cols = slice(TILE * j, TILE * j + TILE)
            to = slice(D + TILE * j, D + TILE * j + TILE)
            values = jnp.concatenate([pairs[at, to] for at in places], axis=0)
            values = jnp.concatenate([values, jnp.ones_like(values)], axis=1)
            weight = jnp.concatenate(
                [weights(score[:TILE], 2 * j), weights(score[TILE:], 2 * j + 1)], axis=0
            )
            got = dot(weight, values)
            num = acc[0, rows, cols] + jnp.where(half, got[:TILE, :TILE], got[TILE:, :TILE])
            den = acc[1, rows, cols] + jnp.where(half, got[:TILE, TILE:], got[TILE:, TILE:])
            mixed = num / den
            hidden[rows, cols] = (0.5 * mixed * (1.0 + lax.erf(mixed * math.sqrt(0.5)))).astype(BF16)
            score = ahead

    def tile_body(a, carry):
        wide = counts[a, 4] + counts[a, 5] + counts[a, 6] + counts[a, 7] > 0

        @pl.when(wide)
        def _():
            tile_block(a, 8)

        @pl.when(jnp.logical_not(wide))
        def _():
            tile_block(a, 4)

        return carry

    lax.fori_loop(0, 4, tile_body, 0)

    for a in range(2):
        rows = slice(256 * a, 256 * a + 256)
        projected = dot(hidden[rows, :], output_w[...])
        blended = alpha * projected + (1.0 - alpha) * papers[rows, :].astype(F32)
        centre = jnp.mean(blended, axis=1, keepdims=True)
        blended = blended - centre
        spread = jnp.mean(jnp.square(blended), axis=1, keepdims=True)
        updated[rows, :] = (blended * lax.rsqrt(spread + 1e-05) * gain[...]).astype(BF16)


def per_device(
    papers,
    cited_rows,
    entities,
    entity_kinds,
    query_weight,
    key_weight,
    value_weight,
    attention_rel,
    message_rel,
    relation_prior,
    output_weight,
    skip_gate,
    norm_gain,
    cite_pattern,
    cite_tiles,
    cite_counts,
    entity_pattern,
    entity_tiles,
    entity_counts,
):
    vmem = pl.BlockSpec(memory_space=pltpu.VMEM)
    smem = pl.BlockSpec(memory_space=pltpu.SMEM)
    shape = jax.ShapeDtypeStruct
    tie = lax.optimization_barrier

    def call(kernel, outs, ins, mib, flops, name, scratch=()):
        return pl.pallas_call(
            kernel,
            out_shape=outs,
            in_specs=ins,
            out_specs=jax.tree.map(lambda _: vmem, outs),
            scratch_shapes=scratch,
            compiler_params=pltpu.CompilerParams(vmem_limit_bytes=mib * 2**20),
            cost_estimate=pl.CostEstimate(
                flops=flops * 10**9, bytes_accessed=8 * 2**20, transcendentals=0
            ),
            name=name,
        )

    def up(value):
        return send(value, lambda x, y, z, c: (x, y, z + 1, c))

    def down(value):
        return send(value, lambda x, y, z, c: (x, y, z - 1, c))

    kinds = jnp.broadcast_to(entity_kinds.astype(BF16)[:, None], (TILE, TILE))
    ent_own = jnp.concatenate([entities, kinds], axis=1)
    a1, b1 = down(cited_rows), up(cited_rows)
    ent_x = send(ent_own, hi_move)
    a1, b1, ent_x, key_weight = tie((a1, b1, ent_x, key_weight))
    ent_pair = jnp.concatenate([ent_own, ent_x], axis=0)
    a2, b2 = down(a1), up(b1)
    ent_y = send(ent_pair, lambda x, y, z, c: (x, y ^ 1, z, c))
    cite_w, own_w, ent_w = call(
        fold_kernel,
        (shape((D, 2 * D), BF16), shape((D, 2 * D), BF16), shape((2 * D, 2 * D), BF16)),
        [vmem] * 4,
        20,
        3,
        "fold_maps",
        [pltpu.VMEM((2, 4, 2, 256, 256), BF16)],
    )(key_weight, value_weight, attention_rel, message_rel)
    a2, b2, cite_w = tie((a2, b2, cite_w))
    first = jnp.concatenate([cited_rows, a1, b1, a2], axis=0)
    a3, b3 = down(a2), up(b2)
    far_first = send(first, x_up)
    ent_four = jnp.concatenate([ent_pair, ent_y], axis=0)
    a3, b3, ent_four = tie((a3, b3, ent_four))
    ent_rest = send(ent_four, lambda x, y, z, c: (x, 3 - y, z, c))
    a4 = down(a3)
    second = jnp.concatenate([b2, a3], axis=0)
    far_second = send(second, x_up)
    a4, second = tie((a4, second))
    third = jnp.concatenate([b3, a4], axis=0)
    far_third = send(third, x_down)
    source = call(source_kernel, shape((1024, 2 * D), BF16), [vmem] * 4, 16, 2, "cited_sources")
    near = source(first, second, third, cite_w)
    near_other = send(near, core_move)
    entity_pairs, scales = call(
        entity_kernel,
        (shape((1024, 2 * D), BF16), shape((8, HEADS, TILE), F32)),
        [smem] + [vmem] * 3,
        20,
        2,
        "entity_sources",
    )(relation_prior, ent_four, ent_rest, ent_w)
    far_first, far_second, far_third, entity_pairs = tie(
        (far_first, far_second, far_third, entity_pairs)
    )
    far = source(far_first, far_second, far_third, cite_w)
    far_other = send(far, core_move)
    far, own_w = tie((far, own_w))
    q2, acc = call(
        own_kernel,
        (shape((2, 512, D), BF16), shape((2, 512, D), F32)),
        [vmem] * 3 + [smem],
        16,
        1,
        "own_terms",
    )(papers, query_weight, own_w, relation_prior)

    hbm = pl.BlockSpec(memory_space=pl.ANY)
    return call(
        final_kernel,
        shape((512, D), BF16),
        [smem] * 6 + [hbm] * 5 + [vmem] * 8,
        FINAL_MIB,
        4,
        "attend_and_finish",
        [
            pltpu.VMEM((5120, 2 * D), BF16),
            pltpu.VMEM((512, D), BF16),
            pltpu.SemaphoreType.DMA((5,)),
        ],
    )(
        cite_tiles,
        cite_counts,
        entity_tiles.T,
        entity_counts.T,
        relation_prior,
        skip_gate,
        near,
        near_other,
        far,
        far_other,
        entity_pairs,
        scales,
        q2,
        acc,
        cite_pattern,
        entity_pattern,
        papers,
        output_weight,
        norm_gain.reshape(1, D),
    )


def solution(mesh):
    split = P(("paper", "type"))
    in_specs = (
        P(("paper", "type"), None),
        P("paper", None),
        P("type", None),
        P("type"),
        P(),
        P(),
        P(),
        P(),
        P(),
        P(),
        P(),
        P(),
        P(),
        split,
        split,
        split,
        split,
        split,
        split,
    )
    return jax.shard_map(
        per_device, mesh=mesh, in_specs=in_specs, out_specs=P(("paper", "type"), None), check_vma=False
    )
```

```python
import functools
import math

import jax
import jax.numpy as jnp
from jax import lax
from jax.experimental import pallas as pl
from jax.experimental.pallas import tpu as pltpu
from jax.sharding import PartitionSpec as P

CAP = 20.0
D = 512
HEADS = 8
TILE = 128
PAIRS = 4
F32 = jnp.float32
BF16 = jnp.bfloat16
LOG2E = 1.4426950408889634
ZS, YS, XS = 8, 4, 4
FINAL_MIB = 24
FOLD_MIB = 58


def device_index(x, y, z, core):
    x_hi, x_lo = x // 2, x % 2
    return (x_lo * 16 + z * 2 + core) * 8 + (y * 2 + x_hi)


def permutation(move):
    pairs = []
    for x in range(XS):
        for y in range(YS):
            for z in range(ZS):
                for core in range(2):
                    tx, ty, tz, tc = move(x, y, z, core)
                    pairs.append(
                        (device_index(x, y, z, core), device_index(tx % XS, ty % YS, tz % ZS, tc))
                    )
    return pairs


def send(value, move):
    return lax.ppermute(value, ("paper", "type"), permutation(move))


def core_move(x, y, z, c):
    return (x, y, z, 1 - c)


def x_up(x, y, z, c):
    return (x - 1, y, z, c)


def x_down(x, y, z, c):
    return (x + 1, y, z, c)


def hi_move(x, y, z, c):
    return ({0: 3, 3: 0, 1: 2, 2: 1}[x], y, z, c)


def dot(a, b):
    return lax.dot_general(a, b, (((1,), (0,)), ((), ())), preferred_element_type=F32)


def dot_t(a, b):
    return lax.dot_general(a, b, (((1,), (1,)), ((), ())), preferred_element_type=F32)


def iota(shape, dim):
    return lax.broadcasted_iota(jnp.int32, shape, dim)


def low_half(rows):
    return (iota((rows, TILE), 1) & 64) == 0


def head_scale(prior, relation, j):
    return jnp.where(low_half(1), prior[relation, 2 * j], prior[relation, 2 * j + 1]) * (0.125 / CAP)


def mask_of(pattern, a, k, live):
    return jnp.where((pattern[a, k] > 0) & live, 1.0, 0.0).astype(BF16)


def fold_kernel(
    key_in, value_in, att_in, msg_in, cite_w, own_w, ent_w, key_w, value_w, att, msg, blocks, sems
):
    copies = []
    for source, target in ((att_in, att), (msg_in, msg), (key_in, key_w), (value_in, value_w)):
        made = pltpu.make_async_copy(source, target, sems.at[len(copies)])
        made.start()
        copies.append(made)
    copies[0].wait()
    copies[1].wait()
    lane = iota((64, 256), 1)
    row = iota((64, 256), 0)
    for i in range(4):
        place = (lane == row + 64 * i).astype(F32).astype(BF16)
        for t, rel in enumerate((att, msg)):
            for r in range(4):
                for g in range(2):
                    blocks[t, r, g, 64 * i : 64 * i + 64, :] = dot(rel[r, 4 * g + i], place).astype(
                        BF16
                    )
    for t, weight in enumerate((key_w, value_w)):
        copies[2 + t].wait()
        for g in range(2):
            cols = slice(256 * g, 256 * g + 256)
            base = weight[0, :, cols]
            to = slice(512 * t + 256 * g, 512 * t + 256 * g + 256)
            cite_w[:, to] = dot(base, blocks[t, 0, g]).astype(BF16)
            own_w[:, to] = dot(base, blocks[t, 3, g]).astype(BF16)
            for u in range(2):
                ent_w[512 * u : 512 * u + 512, to] = dot(
                    weight[1 + u, :, cols], blocks[t, 1 + u, g]
                ).astype(BF16)


def own_kernel(papers, query_w, own_w, prior, q2, acc):
    half = low_half(1)
    zero = jnp.zeros((1, TILE), BF16)
    sums = ((iota((TILE, TILE), 0) & 64) == (iota((TILE, TILE), 1) & 64)).astype(F32).astype(BF16)
    rows = papers[...]
    for g in range(2):
        cols = slice(256 * g, 256 * g + 256)
        q_pairs = dot(rows, query_w[:, cols]).astype(BF16)
        k_pairs = dot(rows, own_w[:, cols]).astype(BF16)
        v_pairs = dot(rows, own_w[:, 512 + 256 * g : 512 + 256 * g + 256]).astype(BF16)
        for i in range(2):
            j = 2 * g + i
            part = slice(TILE * i, TILE * i + TILE)
            q, k, v = q_pairs[:, part], k_pairs[:, part], v_pairs[:, part]
            cols = slice(TILE * j, TILE * j + TILE)
            q2[0, :, cols] = jnp.where(half, q, zero)
            q2[1, :, cols] = jnp.where(half, zero, q)
            product = q.astype(F32) * k.astype(F32)
            high = product.astype(BF16)
            low = (product - high.astype(F32)).astype(BF16)
            score = dot(high, sums) + dot(low, sums)
            weight = jnp.exp2(jnp.tanh(score * head_scale(prior, 3, j)) * (CAP * LOG2E))
            acc[0, :, cols] = weight.astype(BF16).astype(F32) * v.astype(F32)
            acc[1, :, cols] = weight


def source_kernel(part0, part1, part2, cite_w, pairs):
    base = 0
    for part in (part0, part1, part2):
        rows = part[...]
        at = slice(base, base + rows.shape[0])
        for n in range(4):
            pairs[at, 256 * n : 256 * n + 256] = dot(rows, cite_w[:, 256 * n : 256 * n + 256]).astype(
                BF16
            )
        base += rows.shape[0]


def entity_kernel(prior, ent0, ent1, near, near_other, ent_w, pairs, scales, sems):
    copies = []
    for at, source in enumerate((near, near_other)):
        made = pltpu.make_async_copy(source, pairs.at[pl.ds(1024 * at, 1024)], sems.at[at])
        made.start()
        copies.append(made)
    type_at = lax.axis_index("type")
    y_at, hi_at = type_at // 2, type_at % 2
    pick = (iota((8, TILE), 1) == 0).astype(F32).astype(BF16)
    for s, part in enumerate((ent0, ent1)):
        rows = part[:, :D]
        kind = part[:, D : D + TILE]
        kind4 = jnp.concatenate([kind] * 4, axis=1)
        split = jnp.concatenate([rows * (1 - kind4), rows * kind4], axis=1)
        places = []
        for i in range(4):
            y = y_at if s == 0 else 3 - y_at
            y = y if i < 2 else y + 1 - 2 * (y % 2)
            places.append(y * 2 + (hi_at if i % 2 == 0 else 1 - hi_at))
        for n in range(4):
            made = dot(split, ent_w[:, 256 * n : 256 * n + 256]).astype(BF16)
            for t in range(4):
                at = pl.ds(pl.multiple_of(4096 + places[t] * TILE, TILE), TILE)
                pairs[at, 256 * n : 256 * n + 256] = made[TILE * t : TILE * t + TILE]
        for t in range(4):
            kind_row = dot_t(pick, kind[TILE * t : TILE * t + TILE])[0:1]
            for h in range(HEADS):
                scales[places[t], h : h + 1, :] = jnp.where(
                    kind_row < 0.5, prior[1, h], prior[2, h]
                ) * (0.125 / CAP)
    for made in copies:
        made.wait()


def final_kernel(
    tiles,
    counts,
    entity_tiles,
    entity_counts,
    prior,
    gate,
    far,
    far_other,
    pairs_in,
    scales,
    q2,
    acc,
    pattern,
    entity_pattern,
    papers,
    output_w,
    gain,
    updated,
    pairs,
    hidden,
    sems,
):
    copies = []
    for at, source in enumerate((far, far_other)):
        made = pltpu.make_async_copy(source, pairs.at[pl.ds(2048 + 1024 * at, 1024)], sems.at[at])
        made.start()
        copies.append(made)
    paper_at = lax.axis_index("paper")
    x_lo, z_at, core = paper_at // 16, (paper_at // 2) % ZS, paper_at % 2
    half = low_half(1)
    alpha = jax.nn.sigmoid(jnp.full((1, D), gate[0], F32))

    def place(tile):
        far = jnp.where(tile // 16 == x_lo, 0, 2048)
        other = jnp.where(tile % 2 == core, 0, 1024)
        ahead = ((tile // 2) % ZS + ZS - z_at) % ZS
        at = jnp.where(ahead > 4, 2 * (ZS - ahead), jnp.maximum(2 * ahead - 1, 0))
        return far + other + at * TILE

    for made in copies:
        made.wait()

    def tile_block(a, width):
        rows = pl.ds(pl.multiple_of(a * TILE, TILE), TILE)
        nodes = [entity_tiles[k, a] for k in range(2)]
        starts = [place(tiles[a, k]) for k in range(width)] + [4096 + n * TILE for n in nodes]
        places = [pl.ds(pl.multiple_of(at, TILE), TILE) for at in starts]
        mask = jnp.concatenate(
            [mask_of(pattern, a, k, counts[a, k] > 0) for k in range(width)]
            + [mask_of(entity_pattern, a, k, entity_counts[k, a] > 0) for k in range(2)],
            axis=1,
        )

        total = (width + 2) * TILE
        work = [(j, at) for j in range(PAIRS) for at in range(0, total, 256)]
        scale_rows = [
            jnp.concatenate(
                [jnp.full((1, width * TILE), prior[0, h] * (0.125 / CAP), F32)]
                + [scales[n, h : h + 1, :] for n in nodes],
                axis=1,
            )
            for h in range(HEADS)
        ]

        def sources(cols):
            return jnp.concatenate([pairs[at, cols] for at in places], axis=0)

        keys = [sources(slice(TILE * j, TILE * j + TILE)) for j in range(PAIRS)]

        def scores(j, at):
            cols = slice(TILE * j, TILE * j + TILE)
            both = jnp.concatenate([q2[0, rows, cols], q2[1, rows, cols]], axis=0)
            return dot_t(both, keys[j][at : at + 256])

        def weights(score, h, at):
            scale = scale_rows[h][:, at : at + 256]
            weight = jnp.exp2(jnp.tanh(score * scale) * (CAP * LOG2E))
            return weight.astype(BF16) * mask[:, at : at + 256]

        waiting = [scores(*item) for item in work[:2]]
        made = []
        for n, (j, at) in enumerate(work):
            if n + 2 < len(work):
                waiting.append(scores(*work[n + 2]))
            score = waiting.pop(0)
            made.append(
                jnp.concatenate(
                    [weights(score[:TILE], 2 * j, at), weights(score[TILE:], 2 * j + 1, at)], axis=0
                )
            )
            if at + 256 < total:
                continue
            cols = slice(TILE * j, TILE * j + TILE)
            values = sources(slice(D + TILE * j, D + TILE * j + TILE))
            values = jnp.concatenate([values, jnp.ones_like(values)], axis=1)
            got = dot(jnp.concatenate(made, axis=1), values)
            made = []
            num = acc[0, rows, cols] + jnp.where(half, got[:TILE, :TILE], got[TILE:, :TILE])
            den = acc[1, rows, cols] + jnp.where(half, got[:TILE, TILE:], got[TILE:, TILE:])
            mixed = num / den
            hidden[rows, cols] = (0.5 * mixed * (1.0 + lax.erf(mixed * math.sqrt(0.5)))).astype(BF16)

    def tile_body(a, carry):
        wide = counts[a, 4] + counts[a, 5] + counts[a, 6] + counts[a, 7] > 0

        @pl.when(wide)
        def _():
            tile_block(a, 8)

        @pl.when(jnp.logical_not(wide))
        def _():
            tile_block(a, 4)

        return carry

    lax.fori_loop(0, 4, tile_body, 0)

    for a in range(2):
        rows = slice(256 * a, 256 * a + 256)
        projected = dot(hidden[rows, :], output_w[...])
        blended = alpha * projected + (1.0 - alpha) * papers[rows, :].astype(F32)
        centre = jnp.mean(blended, axis=1, keepdims=True)
        blended = blended - centre
        spread = jnp.mean(jnp.square(blended), axis=1, keepdims=True)
        updated[rows, :] = (blended * lax.rsqrt(spread + 1e-05) * gain[...]).astype(BF16)


def per_device(
    papers,
    cited_rows,
    entities,
    entity_kinds,
    query_weight,
    key_weight,
    value_weight,
    attention_rel,
    message_rel,
    relation_prior,
    output_weight,
    skip_gate,
    norm_gain,
    cite_pattern,
    cite_tiles,
    cite_counts,
    entity_pattern,
    entity_tiles,
    entity_counts,
):
    vmem = pl.BlockSpec(memory_space=pltpu.VMEM)
    smem = pl.BlockSpec(memory_space=pltpu.SMEM)
    shape = jax.ShapeDtypeStruct
    tie = lax.optimization_barrier

    def call(kernel, outs, ins, mib, flops, name, scratch=(), aliases=None):
        return pl.pallas_call(
            kernel,
            out_shape=outs,
            in_specs=ins,
            out_specs=jax.tree.map(lambda _: vmem, outs),
            scratch_shapes=scratch,
            input_output_aliases=aliases or {},
            compiler_params=pltpu.CompilerParams(vmem_limit_bytes=mib * 2**20),
            cost_estimate=pl.CostEstimate(
                flops=flops * 10**9, bytes_accessed=8 * 2**20, transcendentals=0
            ),
            name=name,
        )

    def up(value):
        return send(value, lambda x, y, z, c: (x, y, z + 1, c))

    def down(value):
        return send(value, lambda x, y, z, c: (x, y, z - 1, c))

    kinds = jnp.broadcast_to(entity_kinds.astype(BF16)[:, None], (TILE, TILE))
    ent_own = jnp.concatenate([entities, kinds], axis=1)
    a1, b1 = down(cited_rows), up(cited_rows)
    a1, b1, ent_own, key_weight = tie((a1, b1, ent_own, key_weight))
    a2, b2 = down(a1), up(b1)
    ent_x = send(ent_own, hi_move)
    fixed = pl.BlockSpec(memory_space=pltpu.HBM)
    cite_w, own_w, ent_w = call(
        fold_kernel,
        (shape((D, 2 * D), BF16), shape((D, 2 * D), BF16), shape((2 * D, 2 * D), BF16)),
        [fixed] * 4,
        FOLD_MIB,
        3,
        "fold_maps",
        [
            pltpu.VMEM((3, D, D), BF16),
            pltpu.VMEM((3, D, D), BF16),
            pltpu.VMEM((4, HEADS, 64, 64), BF16),
            pltpu.VMEM((4, HEADS, 64, 64), BF16),
            pltpu.VMEM((2, 4, 2, 256, 256), BF16),
            pltpu.SemaphoreType.DMA((4,)),
        ],
    )(key_weight, value_weight, attention_rel, message_rel)
    a2, b2, ent_x, cite_w, own_w = tie((a2, b2, ent_x, cite_w, own_w))
    first = jnp.concatenate([cited_rows, a1, b1, a2], axis=0)
    a3, b3 = down(a2), up(b2)
    far_first = send(first, x_up)
    ent_pair = jnp.concatenate([ent_own, ent_x], axis=0)
    ent_y = send(ent_pair, lambda x, y, z, c: (x, y ^ 1, z, c))
    ent_four = jnp.concatenate([ent_pair, ent_y], axis=0)
    a3, b3 = tie((a3, b3))
    a4 = down(a3)
    second = jnp.concatenate([b2, a3], axis=0)
    far_second = send(second, x_up)
    ent_rest = send(ent_four, lambda x, y, z, c: (x, 3 - y, z, c))
    a4, second = tie((a4, second))
    third = jnp.concatenate([b3, a4], axis=0)
    far_third = send(third, x_down)
    source = call(source_kernel, shape((1024, 2 * D), BF16), [vmem] * 4, 16, 2, "cited_sources")
    near_third, far_first = tie((third, far_first))
    near = source(first, second, near_third, cite_w)
    near_other = send(near, core_move)
    near_tied, own_w = tie((near, own_w))
    q2, acc = call(
        own_kernel,
        (shape((2, 512, D), BF16), shape((2, 512, D), F32)),
        [vmem] * 3 + [smem],
        16,
        1,
        "own_terms",
    )(papers, query_weight, own_w, relation_prior)
    far_first, far_second, far_third, near, ent_rest, q2 = tie(
        (far_first, far_second, far_third, near_tied, ent_rest, q2)
    )
    far = source(far_first, far_second, far_third, cite_w)
    far_other = send(far, core_move)
    far, near_other = tie((far, near_other))
    pairs, scales = call(
        entity_kernel,
        (shape((5120, 2 * D), BF16), shape((8, HEADS, TILE), F32)),
        [smem] + [vmem] * 2 + [pl.BlockSpec(memory_space=pl.ANY)] * 2 + [vmem],
        20,
        2,
        "entity_sources",
        [pltpu.SemaphoreType.DMA((2,))],
    )(relation_prior, ent_four, ent_rest, near, near_other, ent_w)

    hbm = pl.BlockSpec(memory_space=pl.ANY)
    updated, _ = call(
        final_kernel,
        (shape((512, D), BF16), shape((5120, 2 * D), BF16)),
        [smem] * 6 + [hbm] * 2 + [vmem] * 9,
        FINAL_MIB,
        4,
        "attend_and_finish",
        [pltpu.VMEM((512, D), BF16), pltpu.SemaphoreType.DMA((2,))],
        {8: 1},
    )(
        cite_tiles,
        cite_counts,
        entity_tiles.T,
        entity_counts.T,
        relation_prior,
        skip_gate,
        far,
        far_other,
        pairs,
        scales,
        q2,
        acc,
        cite_pattern,
        entity_pattern,
        papers,
        output_weight,
        norm_gain.reshape(1, D),
    )
    return updated


def solution(mesh):
    split = P(("paper", "type"))
    in_specs = (
        P(("paper", "type"), None),
        P("paper", None),
        P("type", None),
        P("type"),
        P(),
        P(),
        P(),
        P(),
        P(),
        P(),
        P(),
        P(),
        P(),
        split,
        split,
        split,
        split,
        split,
        split,
    )
    return jax.shard_map(
        per_device, mesh=mesh, in_specs=in_specs, out_specs=P(("paper", "type"), None), check_vma=False
    )
```

```python
import functools
import math

import jax
import jax.numpy as jnp
from jax import lax
from jax.experimental import pallas as pl
from jax.experimental.pallas import tpu as pltpu
from jax.sharding import PartitionSpec as P

CAP = 20.0
D = 512
HEADS = 8
TILE = 128
PAIRS = 4
F32 = jnp.float32
BF16 = jnp.bfloat16
LOG2E = 1.4426950408889634
ZS, YS, XS = 8, 4, 4
FINAL_MIB = 24
FOLD_MIB = 58


def device_index(x, y, z, core):
    x_hi, x_lo = x // 2, x % 2
    return (x_lo * 16 + z * 2 + core) * 8 + (y * 2 + x_hi)


def permutation(move):
    pairs = []
    for x in range(XS):
        for y in range(YS):
            for z in range(ZS):
                for core in range(2):
                    tx, ty, tz, tc = move(x, y, z, core)
                    pairs.append(
                        (device_index(x, y, z, core), device_index(tx % XS, ty % YS, tz % ZS, tc))
                    )
    return pairs


def send(value, move):
    return lax.ppermute(value, ("paper", "type"), permutation(move))


def core_move(x, y, z, c):
    return (x, y, z, 1 - c)


def x_up(x, y, z, c):
    return (x - 1, y, z, c)


def x_down(x, y, z, c):
    return (x + 1, y, z, c)


def hi_move(x, y, z, c):
    return ({0: 3, 3: 0, 1: 2, 2: 1}[x], y, z, c)


def dot(a, b):
    return lax.dot_general(a, b, (((1,), (0,)), ((), ())), preferred_element_type=F32)


def dot_t(a, b):
    return lax.dot_general(a, b, (((1,), (1,)), ((), ())), preferred_element_type=F32)


def iota(shape, dim):
    return lax.broadcasted_iota(jnp.int32, shape, dim)


def low_half(rows):
    return (iota((rows, TILE), 1) & 64) == 0


def head_scale(prior, relation, j):
    return jnp.where(low_half(1), prior[relation, 2 * j], prior[relation, 2 * j + 1]) * (0.125 / CAP)


def mask_of(pattern, a, k, live):
    return jnp.where((pattern[a, k] > 0) & live, 1.0, 0.0).astype(BF16)


def fold_kernel(
    key_in,
    value_in,
    att_in,
    msg_in,
    cite_out,
    own_out,
    ent_out,
    key_w,
    value_w,
    att,
    msg,
    blocks,
    cite_w,
    own_w,
    ent_w,
    sems,
):
    copies = []
    for source, target in ((att_in, att), (msg_in, msg), (key_in, key_w), (value_in, value_w)):
        made = pltpu.make_async_copy(source, target, sems.at[len(copies)])
        made.start()
        copies.append(made)
    copies[0].wait()
    copies[1].wait()
    lane = iota((64, 256), 1)
    row = iota((64, 256), 0)
    for i in range(4):
        place = (lane == row + 64 * i).astype(F32).astype(BF16)
        for t, rel in enumerate((att, msg)):
            for r in range(4):
                for g in range(2):
                    blocks[t, r, g, 64 * i : 64 * i + 64, :] = dot(rel[r, 4 * g + i], place).astype(
                        BF16
                    )
    for t, weight in enumerate((key_w, value_w)):
        copies[2 + t].wait()
        for g in range(2):
            cols = slice(256 * g, 256 * g + 256)
            base = weight[0, :, cols]
            to = slice(512 * t + 256 * g, 512 * t + 256 * g + 256)
            cite_w[:, to] = dot(base, blocks[t, 0, g]).astype(BF16)
            own_w[:, to] = dot(base, blocks[t, 3, g]).astype(BF16)
            for u in range(2):
                ent_w[512 * u : 512 * u + 512, to] = dot(
                    weight[1 + u, :, cols], blocks[t, 1 + u, g]
                ).astype(BF16)
        cols = pl.ds(512 * t, 512)
        for source, target in ((cite_w, cite_out), (own_w, own_out), (ent_w, ent_out)):
            made = pltpu.make_async_copy(
                source.at[:, cols], target.at[:, cols], sems.at[len(copies)]
            )
            made.start()
            copies.append(made)
    for made in copies[4:]:
        made.wait()


def own_kernel(papers, query_w, own_w, prior, q2, acc):
    half = low_half(1)
    zero = jnp.zeros((1, TILE), BF16)
    sums = ((iota((TILE, TILE), 0) & 64) == (iota((TILE, TILE), 1) & 64)).astype(F32).astype(BF16)
    rows = papers[...]
    for g in range(2):
        cols = slice(256 * g, 256 * g + 256)
        q_pairs = dot(rows, query_w[:, cols]).astype(BF16)
        k_pairs = dot(rows, own_w[:, cols]).astype(BF16)
        v_pairs = dot(rows, own_w[:, 512 + 256 * g : 512 + 256 * g + 256]).astype(BF16)
        for i in range(2):
            j = 2 * g + i
            part = slice(TILE * i, TILE * i + TILE)
            q, k, v = q_pairs[:, part], k_pairs[:, part], v_pairs[:, part]
            cols = slice(TILE * j, TILE * j + TILE)
            q2[0, :, cols] = jnp.where(half, q, zero)
            q2[1, :, cols] = jnp.where(half, zero, q)
            product = q.astype(F32) * k.astype(F32)
            high = product.astype(BF16)
            low = (product - high.astype(F32)).astype(BF16)
            score = dot(high, sums) + dot(low, sums)
            weight = jnp.exp2(jnp.tanh(score * head_scale(prior, 3, j)) * (CAP * LOG2E))
            acc[0, :, cols] = weight.astype(BF16).astype(F32) * v.astype(F32)
            acc[1, :, cols] = weight


def source_kernel(part0, part1, part2, cite_w, pairs):
    base = 0
    for part in (part0, part1, part2):
        rows = part[...]
        at = slice(base, base + rows.shape[0])
        for n in range(4):
            pairs[at, 256 * n : 256 * n + 256] = dot(rows, cite_w[:, 256 * n : 256 * n + 256]).astype(
                BF16
            )
        base += rows.shape[0]


def entity_kernel(prior, ent0, ent1, near, near_other, ent_w, pairs, scales, sems):
    copies = []
    for at, source in enumerate((near, near_other)):
        made = pltpu.make_async_copy(source, pairs.at[pl.ds(1024 * at, 1024)], sems.at[at])
        made.start()
        copies.append(made)
    type_at = lax.axis_index("type")
    y_at, hi_at = type_at // 2, type_at % 2
    pick = (iota((8, TILE), 1) == 0).astype(F32).astype(BF16)
    for s, part in enumerate((ent0, ent1)):
        rows = part[:, :D]
        kind = part[:, D : D + TILE]
        kind4 = jnp.concatenate([kind] * 4, axis=1)
        split = jnp.concatenate([rows * (1 - kind4), rows * kind4], axis=1)
        places = []
        for i in range(4):
            y = y_at if s == 0 else 3 - y_at
            y = y if i < 2 else y + 1 - 2 * (y % 2)
            places.append(y * 2 + (hi_at if i % 2 == 0 else 1 - hi_at))
        for n in range(4):
            made = dot(split, ent_w[:, 256 * n : 256 * n + 256]).astype(BF16)
            for t in range(4):
                at = pl.ds(pl.multiple_of(4096 + places[t] * TILE, TILE), TILE)
                pairs[at, 256 * n : 256 * n + 256] = made[TILE * t : TILE * t + TILE]
        for t in range(4):
            kind_row = dot_t(pick, kind[TILE * t : TILE * t + TILE])[0:1]
            for h in range(HEADS):
                scales[places[t], h : h + 1, :] = jnp.where(
                    kind_row < 0.5, prior[1, h], prior[2, h]
                ) * (0.125 / CAP)
    for made in copies:
        made.wait()


def final_kernel(
    tiles,
    counts,
    entity_tiles,
    entity_counts,
    prior,
    gate,
    far,
    far_other,
    pairs_in,
    scales,
    q2,
    acc,
    pattern,
    entity_pattern,
    papers,
    output_w,
    gain,
    updated,
    pairs,
    hidden,
    sems,
):
    copies = []
    for at, source in enumerate((far, far_other)):
        made = pltpu.make_async_copy(source, pairs.at[pl.ds(2048 + 1024 * at, 1024)], sems.at[at])
        made.start()
        copies.append(made)
    paper_at = lax.axis_index("paper")
    x_lo, z_at, core = paper_at // 16, (paper_at // 2) % ZS, paper_at % 2
    half = low_half(1)
    alpha = jax.nn.sigmoid(jnp.full((1, D), gate[0], F32))

    def place(tile):
        far = jnp.where(tile // 16 == x_lo, 0, 2048)
        other = jnp.where(tile % 2 == core, 0, 1024)
        ahead = ((tile // 2) % ZS + ZS - z_at) % ZS
        at = jnp.where(ahead > 4, 2 * (ZS - ahead), jnp.maximum(2 * ahead - 1, 0))
        return far + other + at * TILE

    for made in copies:
        made.wait()

    def tile_block(a, width):
        rows = pl.ds(pl.multiple_of(a * TILE, TILE), TILE)
        nodes = [entity_tiles[k, a] for k in range(2)]
        starts = [place(tiles[a, k]) for k in range(width)] + [4096 + n * TILE for n in nodes]
        places = [pl.ds(pl.multiple_of(at, TILE), TILE) for at in starts]
        mask = jnp.concatenate(
            [mask_of(pattern, a, k, counts[a, k] > 0) for k in range(width)]
            + [mask_of(entity_pattern, a, k, entity_counts[k, a] > 0) for k in range(2)],
            axis=1,
        )

        total = (width + 2) * TILE
        work = [(j, at) for j in range(PAIRS) for at in range(0, total, 256)]
        scale_rows = [
            jnp.concatenate(
                [jnp.full((1, width * TILE), prior[0, h] * (0.125 / CAP), F32)]
                + [scales[n, h : h + 1, :] for n in nodes],
                axis=1,
            )
            for h in range(HEADS)
        ]

        def sources(cols):
            return jnp.concatenate([pairs[at, cols] for at in places], axis=0)

        keys = [sources(slice(TILE * j, TILE * j + TILE)) for j in range(PAIRS)]

        def scores(j, at):
            cols = slice(TILE * j, TILE * j + TILE)
            both = jnp.concatenate([q2[0, rows, cols], q2[1, rows, cols]], axis=0)
            return dot_t(both, keys[j][at : at + 256])

        def weights(score, h, at):
            scale = scale_rows[h][:, at : at + 256]
            weight = jnp.exp2(jnp.tanh(score * scale) * (CAP * LOG2E))
            return weight.astype(BF16) * mask[:, at : at + 256]

        waiting = [scores(*item) for item in work[:2]]
        made = []
        for n, (j, at) in enumerate(work):
            if n + 2 < len(work):
                waiting.append(scores(*work[n + 2]))
            score = waiting.pop(0)
            made.append(
                jnp.concatenate(
                    [weights(score[:TILE], 2 * j, at), weights(score[TILE:], 2 * j + 1, at)], axis=0
                )
            )
            if at + 256 < total:
                continue
            cols = slice(TILE * j, TILE * j + TILE)
            values = sources(slice(D + TILE * j, D + TILE * j + TILE))
            values = jnp.concatenate([values, jnp.ones_like(values)], axis=1)
            got = dot(jnp.concatenate(made, axis=1), values)
            made = []
            num = acc[0, rows, cols] + jnp.where(half, got[:TILE, :TILE], got[TILE:, :TILE])
            den = acc[1, rows, cols] + jnp.where(half, got[:TILE, TILE:], got[TILE:, TILE:])
            mixed = num / den
            hidden[rows, cols] = (0.5 * mixed * (1.0 + lax.erf(mixed * math.sqrt(0.5)))).astype(BF16)

    def tile_body(a, carry):
        wide = counts[a, 4] + counts[a, 5] + counts[a, 6] + counts[a, 7] > 0

        @pl.when(wide)
        def _():
            tile_block(a, 8)

        @pl.when(jnp.logical_not(wide))
        def _():
            tile_block(a, 4)

        return carry

    lax.fori_loop(0, 4, tile_body, 0)

    for a in range(2):
        rows = slice(256 * a, 256 * a + 256)
        projected = dot(hidden[rows, :], output_w[...])
        blended = alpha * projected + (1.0 - alpha) * papers[rows, :].astype(F32)
        centre = jnp.mean(blended, axis=1, keepdims=True)
        blended = blended - centre
        spread = jnp.mean(jnp.square(blended), axis=1, keepdims=True)
        updated[rows, :] = (blended * lax.rsqrt(spread + 1e-05) * gain[...]).astype(BF16)


def per_device(
    papers,
    cited_rows,
    entities,
    entity_kinds,
    query_weight,
    key_weight,
    value_weight,
    attention_rel,
    message_rel,
    relation_prior,
    output_weight,
    skip_gate,
    norm_gain,
    cite_pattern,
    cite_tiles,
    cite_counts,
    entity_pattern,
    entity_tiles,
    entity_counts,
):
    vmem = pl.BlockSpec(memory_space=pltpu.VMEM)
    smem = pl.BlockSpec(memory_space=pltpu.SMEM)
    shape = jax.ShapeDtypeStruct
    tie = lax.optimization_barrier

    def call(kernel, outs, ins, mib, flops, name, scratch=(), aliases=None, out_spec=vmem):
        return pl.pallas_call(
            kernel,
            out_shape=outs,
            in_specs=ins,
            out_specs=jax.tree.map(lambda _: out_spec, outs),
            scratch_shapes=scratch,
            input_output_aliases=aliases or {},
            compiler_params=pltpu.CompilerParams(vmem_limit_bytes=mib * 2**20),
            cost_estimate=pl.CostEstimate(
                flops=flops * 10**9, bytes_accessed=8 * 2**20, transcendentals=0
            ),
            name=name,
        )

    def up(value):
        return send(value, lambda x, y, z, c: (x, y, z + 1, c))

    def down(value):
        return send(value, lambda x, y, z, c: (x, y, z - 1, c))

    kinds = jnp.broadcast_to(entity_kinds.astype(BF16)[:, None], (TILE, TILE))
    ent_own = jnp.concatenate([entities, kinds], axis=1)
    a1, b1 = down(cited_rows), up(cited_rows)
    a1, b1, ent_own, key_weight = tie((a1, b1, ent_own, key_weight))
    a2, b2 = down(a1), up(b1)
    ent_x = send(ent_own, hi_move)
    fixed = pl.BlockSpec(memory_space=pltpu.HBM)
    cite_w, own_w, ent_w = call(
        fold_kernel,
        (shape((D, 2 * D), BF16), shape((D, 2 * D), BF16), shape((2 * D, 2 * D), BF16)),
        [fixed] * 4,
        FOLD_MIB,
        3,
        "fold_maps",
        [
            pltpu.VMEM((3, D, D), BF16),
            pltpu.VMEM((3, D, D), BF16),
            pltpu.VMEM((4, HEADS, 64, 64), BF16),
            pltpu.VMEM((4, HEADS, 64, 64), BF16),
            pltpu.VMEM((2, 4, 2, 256, 256), BF16),
            pltpu.VMEM((D, 2 * D), BF16),
            pltpu.VMEM((D, 2 * D), BF16),
            pltpu.VMEM((2 * D, 2 * D), BF16),
            pltpu.SemaphoreType.DMA((10,)),
        ],
        out_spec=pl.BlockSpec(memory_space=pl.ANY),
    )(key_weight, value_weight, attention_rel, message_rel)
    a2, b2, ent_x, cite_w, own_w = tie((a2, b2, ent_x, cite_w, own_w))
    first = jnp.concatenate([cited_rows, a1, b1, a2], axis=0)
    a3, b3 = down(a2), up(b2)
    far_first = send(first, x_up)
    ent_pair = jnp.concatenate([ent_own, ent_x], axis=0)
    ent_y = send(ent_pair, lambda x, y, z, c: (x, y ^ 1, z, c))
    ent_four = jnp.concatenate([ent_pair, ent_y], axis=0)
    a3, b3 = tie((a3, b3))
    a4 = down(a3)
    second = jnp.concatenate([b2, a3], axis=0)
    far_second = send(second, x_down)
    ent_rest = send(ent_four, lambda x, y, z, c: (x, 3 - y, z, c))
    a4, second = tie((a4, second))
    third = jnp.concatenate([b3, a4], axis=0)
    far_third = send(third, x_up)
    source = call(source_kernel, shape((1024, 2 * D), BF16), [vmem] * 4, 16, 2, "cited_sources")
    own_third, own_w = tie((third, own_w))
    q2, acc = call(
        own_kernel,
        (shape((2, 512, D), BF16), shape((2, 512, D), F32)),
        [vmem] * 3 + [smem],
        16,
        1,
        "own_terms",
    )(papers, query_weight, own_w, relation_prior)
    near_third, far_first, q2 = tie((own_third, far_first, q2))
    near = source(first, second, near_third, cite_w)
    near_other = send(near, core_move)
    far_first, far_second, far_third, near, ent_rest = tie(
        (far_first, far_second, far_third, near, ent_rest)
    )
    far = source(far_first, far_second, far_third, cite_w)
    far_other = send(far, core_move)
    far, near_other = tie((far, near_other))
    pairs, scales = call(
        entity_kernel,
        (shape((5120, 2 * D), BF16), shape((8, HEADS, TILE), F32)),
        [smem] + [vmem] * 2 + [pl.BlockSpec(memory_space=pl.ANY)] * 2 + [vmem],
        20,
        2,
        "entity_sources",
        [pltpu.SemaphoreType.DMA((2,))],
    )(relation_prior, ent_four, ent_rest, near, near_other, ent_w)

    hbm = pl.BlockSpec(memory_space=pl.ANY)
    updated, _ = call(
        final_kernel,
        (shape((512, D), BF16), shape((5120, 2 * D), BF16)),
        [smem] * 6 + [hbm] * 2 + [vmem] * 9,
        FINAL_MIB,
        4,
        "attend_and_finish",
        [pltpu.VMEM((512, D), BF16), pltpu.SemaphoreType.DMA((2,))],
        {8: 1},
    )(
        cite_tiles,
        cite_counts,
        entity_tiles.T,
        entity_counts.T,
        relation_prior,
        skip_gate,
        far,
        far_other,
        pairs,
        scales,
        q2,
        acc,
        cite_pattern,
        entity_pattern,
        papers,
        output_weight,
        norm_gain.reshape(1, D),
    )
    return updated


def solution(mesh):
    split = P(("paper", "type"))
    in_specs = (
        P(("paper", "type"), None),
        P("paper", None),
        P("type", None),
        P("type"),
        P(),
        P(),
        P(),
        P(),
        P(),
        P(),
        P(),
        P(),
        P(),
        split,
        split,
        split,
        split,
        split,
        split,
    )
    return jax.shard_map(
        per_device, mesh=mesh, in_specs=in_specs, out_specs=P(("paper", "type"), None), check_vma=False
    )
```

```python
import functools
import math

import jax
import jax.numpy as jnp
from jax import lax
from jax.experimental import pallas as pl
from jax.experimental.pallas import tpu as pltpu
from jax.sharding import PartitionSpec as P

CAP = 20.0
D = 512
HEADS = 8
TILE = 128
PAIRS = 4
F32 = jnp.float32
BF16 = jnp.bfloat16
LOG2E = 1.4426950408889634
ZS, YS, XS = 8, 4, 4
FINAL_MIB = 24
FOLD_MIB = 58


def device_index(x, y, z, core):
    x_hi, x_lo = x // 2, x % 2
    return (x_lo * 16 + z * 2 + core) * 8 + (y * 2 + x_hi)


def permutation(move):
    pairs = []
    for x in range(XS):
        for y in range(YS):
            for z in range(ZS):
                for core in range(2):
                    tx, ty, tz, tc = move(x, y, z, core)
                    pairs.append(
                        (device_index(x, y, z, core), device_index(tx % XS, ty % YS, tz % ZS, tc))
                    )
    return pairs


def send(value, move):
    return lax.ppermute(value, ("paper", "type"), permutation(move))


def core_move(x, y, z, c):
    return (x, y, z, 1 - c)


def x_up(x, y, z, c):
    return (x - 1, y, z, c)


def x_down(x, y, z, c):
    return (x + 1, y, z, c)


def hi_move(x, y, z, c):
    return ({0: 3, 3: 0, 1: 2, 2: 1}[x], y, z, c)


def dot(a, b):
    return lax.dot_general(a, b, (((1,), (0,)), ((), ())), preferred_element_type=F32)


def dot_t(a, b):
    return lax.dot_general(a, b, (((1,), (1,)), ((), ())), preferred_element_type=F32)


def iota(shape, dim):
    return lax.broadcasted_iota(jnp.int32, shape, dim)


def low_half(rows):
    return (iota((rows, TILE), 1) & 64) == 0


def head_scale(prior, relation, j):
    return jnp.where(low_half(1), prior[relation, 2 * j], prior[relation, 2 * j + 1]) * (0.125 / CAP)


def mask_of(pattern, a, k, live):
    return jnp.where((pattern[a, k] > 0) & live, 1.0, 0.0).astype(BF16)


def fold_kernel(
    key_in,
    value_in,
    att_in,
    msg_in,
    cite_out,
    own_out,
    ent_out,
    key_w,
    value_w,
    att,
    msg,
    blocks,
    cite_w,
    own_w,
    ent_w,
    sems,
):
    copies = []
    for source, target in ((att_in, att), (msg_in, msg), (key_in, key_w), (value_in, value_w)):
        made = pltpu.make_async_copy(source, target, sems.at[len(copies)])
        made.start()
        copies.append(made)
    copies[0].wait()
    copies[1].wait()
    lane = iota((64, 256), 1)
    row = iota((64, 256), 0)
    for i in range(4):
        place = (lane == row + 64 * i).astype(F32).astype(BF16)
        for t, rel in enumerate((att, msg)):
            for r in range(4):
                for g in range(2):
                    blocks[t, r, g, 64 * i : 64 * i + 64, :] = dot(rel[r, 4 * g + i], place).astype(
                        BF16
                    )
    for t, weight in enumerate((key_w, value_w)):
        copies[2 + t].wait()
        for g in range(2):
            cols = slice(256 * g, 256 * g + 256)
            base = weight[0, :, cols]
            to = slice(512 * t + 256 * g, 512 * t + 256 * g + 256)
            cite_w[:, to] = dot(base, blocks[t, 0, g]).astype(BF16)
            own_w[:, to] = dot(base, blocks[t, 3, g]).astype(BF16)
            for u in range(2):
                ent_w[512 * u : 512 * u + 512, to] = dot(
                    weight[1 + u, :, cols], blocks[t, 1 + u, g]
                ).astype(BF16)
        cols = pl.ds(512 * t, 512)
        for source, target in ((cite_w, cite_out), (own_w, own_out), (ent_w, ent_out)):
            made = pltpu.make_async_copy(
                source.at[:, cols], target.at[:, cols], sems.at[len(copies)]
            )
            made.start()
            copies.append(made)
    for made in copies[4:]:
        made.wait()


def own_kernel(papers, query_w, own_w, prior, q2, acc):
    half = low_half(1)
    zero = jnp.zeros((1, TILE), BF16)
    sums = ((iota((TILE, TILE), 0) & 64) == (iota((TILE, TILE), 1) & 64)).astype(F32).astype(BF16)
    rows = papers[...]
    for g in range(2):
        cols = slice(256 * g, 256 * g + 256)
        q_pairs = dot(rows, query_w[:, cols]).astype(BF16)
        k_pairs = dot(rows, own_w[:, cols]).astype(BF16)
        v_pairs = dot(rows, own_w[:, 512 + 256 * g : 512 + 256 * g + 256]).astype(BF16)
        for i in range(2):
            j = 2 * g + i
            part = slice(TILE * i, TILE * i + TILE)
            q, k, v = q_pairs[:, part], k_pairs[:, part], v_pairs[:, part]
            cols = slice(TILE * j, TILE * j + TILE)
            q2[0, :, cols] = jnp.where(half, q, zero)
            q2[1, :, cols] = jnp.where(half, zero, q)
            product = q.astype(F32) * k.astype(F32)
            high = product.astype(BF16)
            low = (product - high.astype(F32)).astype(BF16)
            score = dot(high, sums) + dot(low, sums)
            weight = jnp.exp2(jnp.tanh(score * head_scale(prior, 3, j)) * (CAP * LOG2E))
            acc[0, :, cols] = weight.astype(BF16).astype(F32) * v.astype(F32)
            acc[1, :, cols] = weight


def source_kernel(part0, part1, part2, cite_w, pairs):
    base = 0
    for part in (part0, part1, part2):
        rows = part[...]
        at = slice(base, base + rows.shape[0])
        for n in range(4):
            pairs[at, 256 * n : 256 * n + 256] = dot(rows, cite_w[:, 256 * n : 256 * n + 256]).astype(
                BF16
            )
        base += rows.shape[0]


def entity_kernel(prior, ent0, ent1, near, near_other, ent_w, pairs, scales, sems):
    copies = []
    for at, source in enumerate((near, near_other)):
        made = pltpu.make_async_copy(source, pairs.at[pl.ds(1024 * at, 1024)], sems.at[at])
        made.start()
        copies.append(made)
    type_at = lax.axis_index("type")
    y_at, hi_at = type_at // 2, type_at % 2
    pick = (iota((8, TILE), 1) == 0).astype(F32).astype(BF16)
    for s, part in enumerate((ent0, ent1)):
        rows = part[:, :D]
        kind = part[:, D : D + TILE]
        kind4 = jnp.concatenate([kind] * 4, axis=1)
        split = jnp.concatenate([rows * (1 - kind4), rows * kind4], axis=1)
        places = []
        for i in range(4):
            y = y_at if s == 0 else 3 - y_at
            y = y if i < 2 else y + 1 - 2 * (y % 2)
            places.append(y * 2 + (hi_at if i % 2 == 0 else 1 - hi_at))
        for n in range(4):
            made = dot(split, ent_w[:, 256 * n : 256 * n + 256]).astype(BF16)
            for t in range(4):
                at = pl.ds(pl.multiple_of(4096 + places[t] * TILE, TILE), TILE)
                pairs[at, 256 * n : 256 * n + 256] = made[TILE * t : TILE * t + TILE]
        for t in range(4):
            kind_row = dot_t(pick, kind[TILE * t : TILE * t + TILE])[0:1]
            for h in range(HEADS):
                scales[places[t], h : h + 1, :] = jnp.where(
                    kind_row < 0.5, prior[1, h], prior[2, h]
                ) * (0.125 / CAP)
    for made in copies:
        made.wait()


def final_kernel(
    tiles,
    counts,
    entity_tiles,
    entity_counts,
    prior,
    gate,
    far,
    far_other,
    pairs_in,
    scales,
    q2,
    acc,
    pattern,
    entity_pattern,
    papers,
    output_w,
    gain,
    updated,
    pairs,
    hidden,
    sems,
):
    copies = []
    for at, source in enumerate((far, far_other)):
        made = pltpu.make_async_copy(source, pairs.at[pl.ds(2048 + 1024 * at, 1024)], sems.at[at])
        made.start()
        copies.append(made)
    paper_at = lax.axis_index("paper")
    x_lo, z_at, core = paper_at // 16, (paper_at // 2) % ZS, paper_at % 2
    half = low_half(1)
    alpha = jax.nn.sigmoid(gate[...])

    def place(tile):
        far = jnp.where(tile // 16 == x_lo, 0, 2048)
        other = jnp.where(tile % 2 == core, 0, 1024)
        ahead = ((tile // 2) % ZS + ZS - z_at) % ZS
        at = jnp.where(ahead > 4, 2 * (ZS - ahead), jnp.maximum(2 * ahead - 1, 0))
        return far + other + at * TILE

    for made in copies:
        made.wait()

    def tile_block(a, width):
        rows = pl.ds(pl.multiple_of(a * TILE, TILE), TILE)
        nodes = [entity_tiles[k, a] for k in range(2)]
        starts = [place(tiles[a, k]) for k in range(width)] + [4096 + n * TILE for n in nodes]
        places = [pl.ds(pl.multiple_of(at, TILE), TILE) for at in starts]
        mask = jnp.concatenate(
            [mask_of(pattern, a, k, counts[a, k] > 0) for k in range(width)]
            + [mask_of(entity_pattern, a, k, entity_counts[k, a] > 0) for k in range(2)],
            axis=1,
        )

        total = (width + 2) * TILE
        work = [(j, at) for j in range(PAIRS) for at in range(0, total, 256)]
        scale_rows = [
            jnp.concatenate(
                [jnp.full((1, width * TILE), prior[0, h] * (0.125 / CAP), F32)]
                + [scales[n, h : h + 1, :] for n in nodes],
                axis=1,
            )
            for h in range(HEADS)
        ]

        def sources(cols):
            return jnp.concatenate([pairs[at, cols] for at in places], axis=0)

        keys = [sources(slice(TILE * j, TILE * j + TILE)) for j in range(PAIRS)]

        def scores(j, at):
            cols = slice(TILE * j, TILE * j + TILE)
            both = jnp.concatenate([q2[0, rows, cols], q2[1, rows, cols]], axis=0)
            return dot_t(both, keys[j][at : at + 256])

        def weights(score, h, at):
            scale = scale_rows[h][:, at : at + 256]
            weight = jnp.exp2(jnp.tanh(score * scale) * (CAP * LOG2E))
            return weight.astype(BF16) * mask[:, at : at + 256]

        waiting = [scores(*item) for item in work[:2]]
        made = []
        for n, (j, at) in enumerate(work):
            if n + 2 < len(work):
                waiting.append(scores(*work[n + 2]))
            score = waiting.pop(0)
            made.append(
                jnp.concatenate(
                    [weights(score[:TILE], 2 * j, at), weights(score[TILE:], 2 * j + 1, at)], axis=0
                )
            )
            if at + 256 < total:
                continue
            cols = slice(TILE * j, TILE * j + TILE)
            values = sources(slice(D + TILE * j, D + TILE * j + TILE))
            values = jnp.concatenate([values, jnp.ones_like(values)], axis=1)
            got = dot(jnp.concatenate(made, axis=1), values)
            made = []
            num = acc[0, rows, cols] + jnp.where(half, got[:TILE, :TILE], got[TILE:, :TILE])
            den = acc[1, rows, cols] + jnp.where(half, got[:TILE, TILE:], got[TILE:, TILE:])
            mixed = num / den
            hidden[rows, cols] = (0.5 * mixed * (1.0 + lax.erf(mixed * math.sqrt(0.5)))).astype(BF16)

    def tile_body(a, carry):
        wide = counts[a, 4] + counts[a, 5] + counts[a, 6] + counts[a, 7] > 0

        @pl.when(wide)
        def _():
            tile_block(a, 8)

        @pl.when(jnp.logical_not(wide))
        def _():
            tile_block(a, 4)

        return carry

    lax.fori_loop(0, 4, tile_body, 0)

    for a in range(2):
        rows = slice(256 * a, 256 * a + 256)
        projected = dot(hidden[rows, :], output_w[...])
        blended = alpha * projected + (1.0 - alpha) * papers[rows, :].astype(F32)
        centre = jnp.mean(blended, axis=1, keepdims=True)
        blended = blended - centre
        spread = jnp.mean(jnp.square(blended), axis=1, keepdims=True)
        updated[rows, :] = (blended * lax.rsqrt(spread + 1e-05) * gain[...]).astype(BF16)


def per_device(
    papers,
    cited_rows,
    entities,
    entity_kinds,
    query_weight,
    key_weight,
    value_weight,
    attention_rel,
    message_rel,
    relation_prior,
    output_weight,
    skip_gate,
    norm_gain,
    cite_pattern,
    cite_tiles,
    cite_counts,
    entity_pattern,
    entity_tiles,
    entity_counts,
):
    vmem = pl.BlockSpec(memory_space=pltpu.VMEM)
    smem = pl.BlockSpec(memory_space=pltpu.SMEM)
    shape = jax.ShapeDtypeStruct
    tie = lax.optimization_barrier

    def call(kernel, outs, ins, mib, flops, name, scratch=(), aliases=None, out_spec=vmem):
        return pl.pallas_call(
            kernel,
            out_shape=outs,
            in_specs=ins,
            out_specs=jax.tree.map(lambda _: out_spec, outs),
            scratch_shapes=scratch,
            input_output_aliases=aliases or {},
            compiler_params=pltpu.CompilerParams(vmem_limit_bytes=mib * 2**20),
            cost_estimate=pl.CostEstimate(
                flops=flops * 10**9, bytes_accessed=8 * 2**20, transcendentals=0
            ),
            name=name,
        )

    def up(value):
        return send(value, lambda x, y, z, c: (x, y, z + 1, c))

    def down(value):
        return send(value, lambda x, y, z, c: (x, y, z - 1, c))

    kinds = jnp.broadcast_to(entity_kinds.astype(BF16)[:, None], (TILE, TILE))
    ent_own = jnp.concatenate([entities, kinds], axis=1)
    a1, b1 = down(cited_rows), up(cited_rows)
    a1, b1, ent_own, key_weight = tie((a1, b1, ent_own, key_weight))
    a2, b2 = down(a1), up(b1)
    ent_x = send(ent_own, hi_move)
    fixed = pl.BlockSpec(memory_space=pltpu.HBM)
    cite_w, own_w, ent_w = call(
        fold_kernel,
        (shape((D, 2 * D), BF16), shape((D, 2 * D), BF16), shape((2 * D, 2 * D), BF16)),
        [fixed] * 4,
        FOLD_MIB,
        3,
        "fold_maps",
        [
            pltpu.VMEM((3, D, D), BF16),
            pltpu.VMEM((3, D, D), BF16),
            pltpu.VMEM((4, HEADS, 64, 64), BF16),
            pltpu.VMEM((4, HEADS, 64, 64), BF16),
            pltpu.VMEM((2, 4, 2, 256, 256), BF16),
            pltpu.VMEM((D, 2 * D), BF16),
            pltpu.VMEM((D, 2 * D), BF16),
            pltpu.VMEM((2 * D, 2 * D), BF16),
            pltpu.SemaphoreType.DMA((10,)),
        ],
        out_spec=pl.BlockSpec(memory_space=pl.ANY),
    )(key_weight, value_weight, attention_rel, message_rel)
    a2, b2, ent_x, cite_w, own_w = tie((a2, b2, ent_x, cite_w, own_w))
    first = jnp.concatenate([cited_rows, a1, b1, a2], axis=0)
    a3, b3 = down(a2), up(b2)
    far_first = send(first, x_up)
    ent_pair = jnp.concatenate([ent_own, ent_x], axis=0)
    ent_y = send(ent_pair, lambda x, y, z, c: (x, y ^ 1, z, c))
    ent_four = jnp.concatenate([ent_pair, ent_y], axis=0)
    a3, b3, gate_row = tie((a3, b3, jnp.broadcast_to(skip_gate[None], (1, D))))
    a4 = down(a3)
    second = jnp.concatenate([b2, a3], axis=0)
    far_second = send(second, x_down)
    ent_rest = send(ent_four, lambda x, y, z, c: (x, 3 - y, z, c))
    a4, second = tie((a4, second))
    third = jnp.concatenate([b3, a4], axis=0)
    far_third = send(third, x_up)
    source = call(source_kernel, shape((1024, 2 * D), BF16), [vmem] * 4, 16, 2, "cited_sources")
    own_third, own_w = tie((third, own_w))
    q2, acc = call(
        own_kernel,
        (shape((2, 512, D), BF16), shape((2, 512, D), F32)),
        [vmem] * 3 + [smem],
        16,
        1,
        "own_terms",
    )(papers, query_weight, own_w, relation_prior)
    near_third, far_first, q2 = tie((own_third, far_first, q2))
    near = source(first, second, near_third, cite_w)
    near_other = send(near, core_move)
    far_first, far_second, far_third, near, ent_rest = tie(
        (far_first, far_second, far_third, near, ent_rest)
    )
    far = source(far_first, far_second, far_third, cite_w)
    far_other = send(far, core_move)
    far, near_other = tie((far, near_other))
    pairs, scales = call(
        entity_kernel,
        (shape((5120, 2 * D), BF16), shape((8, HEADS, TILE), F32)),
        [smem] + [vmem] * 2 + [pl.BlockSpec(memory_space=pl.ANY)] * 2 + [vmem],
        20,
        2,
        "entity_sources",
        [pltpu.SemaphoreType.DMA((2,))],
    )(relation_prior, ent_four, ent_rest, near, near_other, ent_w)

    hbm = pl.BlockSpec(memory_space=pl.ANY)
    updated, _ = call(
        final_kernel,
        (shape((512, D), BF16), shape((5120, 2 * D), BF16)),
        [smem] * 5 + [vmem] + [hbm] * 2 + [vmem] * 9,
        FINAL_MIB,
        4,
        "attend_and_finish",
        [pltpu.VMEM((512, D), BF16), pltpu.SemaphoreType.DMA((2,))],
        {8: 1},
    )(
        cite_tiles,
        cite_counts,
        entity_tiles.T,
        entity_counts.T,
        relation_prior,
        gate_row,
        far,
        far_other,
        pairs,
        scales,
        q2,
        acc,
        cite_pattern,
        entity_pattern,
        papers,
        output_weight,
        norm_gain.reshape(1, D),
    )
    return updated


def solution(mesh):
    split = P(("paper", "type"))
    in_specs = (
        P(("paper", "type"), None),
        P("paper", None),
        P("type", None),
        P("type"),
        P(),
        P(),
        P(),
        P(),
        P(),
        P(),
        P(),
        P(),
        P(),
        split,
        split,
        split,
        split,
        split,
        split,
    )
    return jax.shard_map(
        per_device, mesh=mesh, in_specs=in_specs, out_specs=P(("paper", "type"), None), check_vma=False
    )
```
